32 devices in a mesh: seq: 4 (over z), batch: 8 (over y, x, core).
Axes of the slice: x: 2, y: 2, z: 4, core: 2. Of those that a mesh axis runs over, the one named last changes fastest.
Arguments:
- tokens: bfloat16 [16, 1024, 2048], P('batch', 'seq'), may hold values from -6 to 6
- segments: int32 [16, 1024], P('batch', 'seq'), may hold values from 0 to 5, as said below
- norm1_gain: float32 [2048], replicated, may hold values from 0.1 to 1.9
- w_query: bfloat16 [2048, 2048], replicated, may hold values from -0.125 to 0.125
- w_key: bfloat16 [2048, 128], replicated, may hold values from -0.125 to 0.125
- w_value: bfloat16 [2048, 128], replicated, may hold values from -0.125 to 0.125
- w_output: bfloat16 [2048, 2048], replicated, may hold values from -1 to 1
- norm2_gain: float32 [2048], replicated, may hold values from 0.1 to 1.9
- w_gate: bfloat16 [2048, 5632], replicated, may hold values from -0.125 to 0.125
- w_up: bfloat16 [2048, 5632], replicated, may hold values from -0.125 to 0.125
- w_down: bfloat16 [5632, 2048], replicated, may hold values from -0.15625 to 0.15625
- cotangent: bfloat16 [16, 1024, 2048], P('batch', 'seq'), may hold values from -6 to 6
Outputs:
- output: bfloat16 [16, 1024, 2048], P('batch', 'seq')
- grad_tokens: float32 [16, 1024, 2048], P('batch', 'seq')
- grad_norm1: float32 [2048], P(('seq', 'batch'))
- grad_query: float32 [2048, 2048], P(('seq', 'batch'))
- grad_key: float32 [2048, 128], P(('seq', 'batch'))
- grad_value: float32 [2048, 128], P(('seq', 'batch'))
- grad_output: float32 [2048, 2048], P(('seq', 'batch'))
- grad_norm2: float32 [2048], P(('seq', 'batch'))
- grad_gate: float32 [2048, 5632], P(('seq', 'batch'))
- grad_up: float32 [2048, 5632], P(('seq', 'batch'))
- grad_down: float32 [5632, 2048], P(('seq', 'batch'))
The draws below stay inside these ranges and needn't reach their ends.
Inputs may be any that keep to these rules, and one draw needn't show every extreme that they name: `segments`: segment ids number the documents of a sequence from 0 upward and never fall along it. Of the 2 sequences on one index of batch, one, drawn from the seed, is a single document; each other one holds 6 documents of random lengths.
All inputs are finite; a program needn't handle non-finite values.
Results may differ from the reference program's by a relative error of at most 0.015.
Values may be sent and summed in bfloat16 or wider, within the bound.
No kernel may reach another device: no remote copies, remote signals or barrier semaphores. Data moves between devices by JAX's collectives and lax.ppermute only.
A program may use at most 448 MiB of HBM per device.

```python
import math
import jax
import jax.numpy as jnp
from jax import lax

D = 2048
NH = 16
HD = 128
FF = 5632
WINDOW = 512
SEQ_GRP = 2
NDOCS = 6
LENGTH = 1024
SEQS = 16


def packed_row(row_key):
    shuffled = jax.random.permutation(row_key, LENGTH - 1) + 1
    cut_points = shuffled[:NDOCS - 1]
    token_index = jnp.arange(LENGTH, dtype=jnp.int32)
    return jnp.sum((token_index[:, None] >= cut_points[None, :]).astype(jnp.int32), axis=1)


def draw_segments(key, part):
    pick_key = jax.random.fold_in(key, 11)
    rows_key = jax.random.fold_in(key, 23)
    single_slot = jax.random.randint(pick_key, (SEQS // SEQ_GRP,), 0, SEQ_GRP)
    row_keys = jax.random.split(rows_key, SEQS)
    packed = jax.vmap(packed_row)(row_keys)
    row_slot = jnp.arange(SEQS, dtype=jnp.int32) % SEQ_GRP
    is_single = row_slot == jnp.repeat(single_slot, SEQ_GRP)
    return jnp.where(is_single[:, None], 0, packed).astype(jnp.int32)


def levels(rng, extent, shards, low, largest):
    def one(position, shards_of):
        heights = jax.random.uniform(jax.random.fold_in(jax.random.fold_in(rng, 6), position), (shards_of,), jnp.float32, low / len(shards), largest / len(shards))
        return jnp.repeat(jnp.exp(heights), extent[position] // shards_of).reshape((-1,) + (1,) * (len(extent) - position - 1))

    factor_of = one(*shards[0])
    for cut in shards[1:]:
        factor_of = factor_of * one(*cut)
    return factor_of


def centred(stream_key, shape, deviation, limit, shards=(), kind=jnp.bfloat16):
    level = levels(stream_key, shape, shards, -0.22, 0.18) if shards else 1.0
    entries = jax.random.normal(stream_key, shape, jnp.float32) * deviation * level
    return jnp.minimum(jnp.maximum(entries, -limit), limit).astype(kind)


def setup_inputs(seed: int = 0) -> dict:
    streams_of = jax.random.split(jax.random.key(seed), 13)
    return {
        "tokens": centred(streams_of[0], (SEQS, LENGTH, D), 1.0, 6.0, ((0, 8), (1, 4))),
        "segments": draw_segments(jax.random.fold_in(streams_of[12], 71), 0),
        "norm1_gain": jnp.clip(1.0 + 0.18 * jax.random.normal(streams_of[2], (D,), jnp.float32), 0.1, 1.9),
        "w_query": centred(streams_of[3], (D, NH * HD), D ** -0.5, 0.125),
        "w_key": centred(streams_of[4], (D, HD), D ** -0.5, 0.125),
        "w_value": centred(streams_of[5], (D, HD), D ** -0.5, 0.125),
        "w_output": centred(streams_of[6], (NH * HD, D), (NH * HD // 64) ** -0.5, 1.0),
        "norm2_gain": jnp.clip(1.0 + 0.18 * jax.random.normal(streams_of[7], (D,), jnp.float32), 0.1, 1.9),
        "w_gate": centred(streams_of[8], (D, FF), D ** -0.5, 0.125),
        "w_up": centred(streams_of[9], (D, FF), D ** -0.5, 0.125),
        "w_down": centred(streams_of[10], (FF, D), (FF // 4) ** -0.5, 0.15625),
        "cotangent": centred(streams_of[11], (SEQS, LENGTH, D), 1.0, 6.0, ((0, 8), (1, 4))),
    }


eps = 1e-05
rope_base = 10000.0
masked = -1e+30
highest = lax.Precision.HIGHEST

@jax.custom_vjp
def low(v):
    return lax.optimization_barrier(v.astype(jnp.bfloat16)).astype(jnp.float32)

@jax.custom_vjp
def low_back(v):
    return v

def low_keep(v):
    return (low(v), None)

def low_pass(kept, grad):
    return (grad,)

def back_keep(v):
    return (v, None)

def back_low(kept, grad):
    return (low(grad),)
low.defvjp(low_keep, low_pass)
low_back.defvjp(back_keep, back_low)

def rope_turn(tensor, positions, sign):
    half = tensor.shape[-1] // 2
    freq = jnp.exp(-math.log(rope_base) * jnp.arange(half, dtype=jnp.float32) / half)
    angle = positions[..., None] * freq
    cosine = jnp.cos(angle)
    sine = sign * jnp.sin(angle)
    first_half = tensor[..., :half]
    second_half = tensor[..., half:]
    return jnp.concatenate([first_half * cosine - second_half * sine, first_half * sine + second_half * cosine], axis=-1)

def rms_scale(rows, gain):
    return rows * lax.rsqrt(lax.optimization_barrier(jnp.mean(rows * rows, axis=-1, keepdims=True)) + eps) * gain

def attend_sequence(queries, key_rot, value_rot, starts):
    length = queries.shape[0]
    block_rows = min(512, length)
    key_span = block_rows + WINDOW
    score_scale = 1.0 / math.sqrt(HD)
    key_pad = jnp.pad(key_rot, ((WINDOW, 0), (0, 0)))
    value_pad = jnp.pad(value_rot, ((WINDOW, 0), (0, 0)))

    def one_block(block_index):
        first = block_index * block_rows
        q_block = lax.dynamic_slice_in_dim(queries, first, block_rows, 0)
        k_block = lax.dynamic_slice_in_dim(key_pad, first, key_span, 0)
        v_block = lax.dynamic_slice_in_dim(value_pad, first, key_span, 0)
        query_index = first + jnp.arange(block_rows, dtype=jnp.int32)
        key_index = first - WINDOW + jnp.arange(key_span, dtype=jnp.int32)
        start_block = lax.dynamic_slice_in_dim(starts, first, block_rows, 0)
        allow = (key_index[None, :] <= query_index[:, None]) & (query_index[:, None] - key_index[None, :] < WINDOW) & (key_index[None, :] >= start_block[:, None])
        raw = low_back(jnp.einsum('qhd,kd->hqk', q_block, k_block, precision=highest))
        scores = jnp.where(allow[None], raw * score_scale, masked)
        top = lax.optimization_barrier(jnp.max(scores, axis=-1, keepdims=True))
        expo = jnp.exp(scores - top)
        probs = low(expo / lax.optimization_barrier(jnp.sum(expo, axis=-1, keepdims=True)))
        return jnp.einsum('hqk,kd->qhd', probs, v_block, precision=highest)
    pieces = lax.map(jax.checkpoint(one_block), jnp.arange(length // block_rows, dtype=jnp.int32))
    return pieces.reshape(length, NH * HD)

def layer_sequence(x_seq, segment_seq, gain_one, wq, wk, wv, wo, gain_two, wg, wu, wd):
    length = x_seq.shape[0]
    token_index = jnp.arange(length, dtype=jnp.int32)
    fresh = jnp.concatenate([jnp.ones((1,), dtype=bool), segment_seq[1:] != segment_seq[:-1]])
    starts = lax.cummax(jnp.where(fresh, token_index, 0), axis=0)
    positions = (token_index - starts).astype(jnp.float32)
    normed = low(rms_scale(x_seq, gain_one))
    query_lin = low_back(jnp.dot(normed, wq, precision=highest)).reshape(length, NH, HD)
    queries = low(rope_turn(query_lin, positions[:, None], 1.0))
    key_rot = low(rope_turn(low_back(jnp.dot(normed, wk, precision=highest)), positions, 1.0))
    value_rot = low(low_back(jnp.dot(normed, wv, precision=highest)))
    attended = low_back(low(attend_sequence(queries, key_rot, value_rot, starts)))
    mid = x_seq + low_back(jnp.dot(attended, wo, precision=highest))
    normed_two = low(rms_scale(mid, gain_two))
    gate_lin = low_back(jnp.dot(normed_two, wg, precision=highest))
    up_lin = low_back(jnp.dot(normed_two, wu, precision=highest))
    hidden = low(jax.nn.silu(gate_lin) * up_lin)
    return mid + low_back(jnp.dot(hidden, wd, precision=highest))

def reference(tokens, segments, norm1_gain, w_query, w_key, w_value, w_output, norm2_gain, w_gate, w_up, w_down, cotangent):

    def forward(x_all, gain_one, wq, wk, wv, wo, gain_two, wg, wu, wd):

        def per_sequence(pair):
            return layer_sequence(pair[0], pair[1], gain_one, wq, wk, wv, wo, gain_two, wg, wu, wd)
        return lax.map(jax.checkpoint(per_sequence), (x_all, segments))
    result, pullback = jax.vjp(forward, tokens.astype(jnp.float32), norm1_gain.astype(jnp.float32), w_query.astype(jnp.float32), w_key.astype(jnp.float32), w_value.astype(jnp.float32), w_output.astype(jnp.float32), norm2_gain.astype(jnp.float32), w_gate.astype(jnp.float32), w_up.astype(jnp.float32), w_down.astype(jnp.float32))
    grads = pullback(cotangent.astype(jnp.float32))
    return (result.astype(jnp.bfloat16), grads[0], grads[1], grads[2], grads[3], grads[4], grads[5], grads[6], grads[7], grads[8], grads[9])
```

```python
import functools
import math

import jax
import jax.numpy as jnp
from jax import lax
from jax.experimental import pallas as pl
from jax.experimental.pallas import tpu as pltpu
from jax.sharding import PartitionSpec as P

WINDOW = 512
eps = 1e-05
rope_base = 10000.0
masked = -1e30
big = 1 << 30
AXES = ("seq", "batch")
GROUP = 4
f32 = jnp.float32
bf16 = jnp.bfloat16


MIB = 2**20
ONCE = pl.Buffered(1)
ANY = pl.BlockSpec(memory_space=pl.ANY)
SCALE = 1.0
COST = dict(
    norm_keys=5, query=9, attend=30, project_out=11, down_back=20, feed=21, gate_send=11, up_send=11, down_send=11,
    gate_keep=12, up_keep=12, down_keep=12, dn2_away=20, dn2_near=22, out_away=11, out_near=13, mid_back=14,
    attend_back=29, w_out_send=7, w_out_keep=7, w_query_send=7, w_query_keep=7, tokens_back=14, output=5,
)


def call(kernel, name, args, deps=(), scalars=(), grid=(1,), in_specs=(), out_specs=None, out_shape=None, scratch=(), vmem=56, passes=()):
    n_s, n_a, n_d, n_p = len(scalars), len(args), len(deps), len(passes)
    several = isinstance(out_shape, (list, tuple))
    shapes, specs = (list(out_shape), list(out_specs)) if several else ([out_shape], [out_specs])
    n_o = len(shapes)

    def body(*refs):
        at = n_s + n_a + n_d + n_p
        kernel(*refs[: n_s + n_a], *refs[at : at + n_o], *refs[at + n_o + n_p :])

    out = pl.pallas_call(
        body,
        grid_spec=pltpu.PrefetchScalarGridSpec(
            num_scalar_prefetch=n_s,
            grid=grid,
            in_specs=list(in_specs) + [ANY] * (n_d + n_p),
            out_specs=specs + [ANY] * n_p,
            scratch_shapes=list(scratch),
        ),
        out_shape=shapes + [jax.ShapeDtypeStruct(p.shape, p.dtype) for p in passes],
        input_output_aliases={n_s + n_a + n_d + i: n_o + i for i in range(n_p)},
        compiler_params=pltpu.CompilerParams(vmem_limit_bytes=vmem * MIB),
        cost_estimate=pl.CostEstimate(flops=int(SCALE * COST[name] * 10**9), bytes_accessed=1, transcendentals=0),
        name=name,
    )(*scalars, *args, *deps, *passes)
    return out if several or passes else out[0]


def dot(a, b, ca, cb, out=f32):
    return lax.dot_general(a, b, (((ca,), (cb,)), ((), ())), preferred_element_type=f32).astype(out)


class Moves:
    def __init__(self):
        self.nz, self.nb = lax.axis_size("seq"), lax.axis_size("batch")
        self.z, self.b = lax.axis_index("seq"), lax.axis_index("batch")
        self.ny = self.nb // GROUP
        self.y = self.b // GROUP

    def flip(self, value, mask):
        nz, nb = self.nz, self.nb
        pairs = [(z * nb + b, z * nb + (b ^ mask)) for z in range(nz) for b in range(nb)]
        return lax.ppermute(value, AXES, pairs)

    def shift(self, value, axis, sources, step):
        nz, ny, nb = self.nz, self.ny, self.nb
        pairs = []
        for z in range(nz):
            for b in range(nb):
                y, q = b // GROUP, b % GROUP
                at, size = (z, nz) if axis == "z" else (y, ny)
                if at in sources and 0 <= at + step < size:
                    to = (z + step, y) if axis == "z" else (z, y + step)
                    pairs.append((z * nb + b, to[0] * nb + to[1] * GROUP + q))
        return lax.ppermute(value, AXES, pairs)

    def bit(self, mask):
        return (self.b // mask) % 2


def turn(u, cosine, sine):
    return u * cosine + pltpu.roll(u, 64, 1) * sine


def mask_bias(starts, rows, first_row, keys, first_key, hop):
    qi = lax.broadcasted_iota(jnp.int32, (rows, keys), 0) + (first_row + hop)
    kj = lax.broadcasted_iota(jnp.int32, (rows, keys), 1) + first_key
    allow = (kj <= qi) & (qi - kj < WINDOW) & (kj >= starts)
    return jnp.where(allow, 0.0, masked)


def fwd_kernel(q_ref, cos_ref, sin_ref, start_ref, k_ref, v_ref, o_ref, qr_ref, lse_ref, *, heads, rb, hop):
    rows = q_ref.shape[0]
    scale = 1.0 / math.sqrt(128)
    lses = []
    for r in range(rows // rb):
        sl = pl.ds(r * rb, rb)
        k0 = max(0, r * rb + hop - WINDOW)
        k0 -= k0 % 128
        k1 = (r + 1) * rb + hop
        bias = mask_bias(start_ref[sl, :], rb, r * rb, k1 - k0, k0, hop)
        cosine, sine = cos_ref[sl, :], sin_ref[sl, :]
        kk = k_ref[0, pl.ds(k0, k1 - k0), :]
        vv = v_ref[0, pl.ds(k0, k1 - k0), :]
        lse_row = []
        for h in range(heads):
            hs = pl.ds(h * 128, 128)
            qr = turn(q_ref[sl, hs], cosine, sine).astype(bf16)
            qr_ref[sl, hs] = qr
            s = dot(qr, kk, 1, 1) * scale + bias
            top = jnp.max(s, axis=1, keepdims=True)
            e = jnp.exp(s - top)
            total = jnp.sum(e, axis=1, keepdims=True)
            p = (e * (1.0 / total)).astype(bf16)
            o_ref[sl, hs] = dot(p, vv, 1, 0).astype(bf16)
            lse_row.append(top + jnp.log(total))
        lses.append(jnp.concatenate(lse_row, axis=1))
    lse_ref[0, 0] = jnp.concatenate(lses, axis=0)


def bwd_kernel(q_ref, o_ref, do_ref, lse_ref, cos_ref, sin_ref, start_ref, k_ref, v_ref, dq_ref, dk_ref, dv_ref, *, heads, rb, hop):
    rows = q_ref.shape[0]
    scale = 1.0 / math.sqrt(128)

    @pl.when(pl.program_id(1) == 0)
    def _():
        dk_ref[...] = jnp.zeros_like(dk_ref)
        dv_ref[...] = jnp.zeros_like(dv_ref)

    for r in range(rows // rb):
        sl = pl.ds(r * rb, rb)
        k0 = max(0, r * rb + hop - WINDOW)
        k0 -= k0 % 128
        k1 = (r + 1) * rb + hop
        ks = pl.ds(k0, k1 - k0)
        bias = mask_bias(start_ref[sl, :], rb, r * rb, k1 - k0, k0, hop)
        cosine, sine = cos_ref[sl, :], sin_ref[sl, :]
        kk, vv = k_ref[0, ks, :], v_ref[0, ks, :]
        dk = dv = None
        for h in range(heads):
            hs = pl.ds(h * 128, 128)
            q, do = q_ref[sl, hs], do_ref[sl, hs]
            inner = jnp.sum(do.astype(f32) * o_ref[sl, hs].astype(f32), axis=1, keepdims=True)
            s = dot(q, kk, 1, 1) * scale + bias
            p = jnp.exp(s - lse_ref[0, 0, sl, h : h + 1])
            dp = dot(do, vv, 1, 1)
            ds = (p * ((dp - inner) * scale)).astype(bf16)
            dq = dot(ds, kk, 1, 0)
            dq_ref[sl, hs] = turn(dq, cosine, -sine).astype(bf16)
            dkh = dot(ds, q, 0, 0)
            dvh = dot(p.astype(bf16), do, 0, 0)
            dk = dkh if dk is None else dk + dkh
            dv = dvh if dv is None else dv + dvh
        dk_ref[0, ks, :] += dk
        dv_ref[0, ks, :] += dv


HEADS = 4
ROWS = 128


def attention_specs(L, span):
    wide = pl.BlockSpec((L, HEADS * 128), lambda s, h: (s, h))
    table = pl.BlockSpec((L, 128), lambda s, h: (s, 0))
    starts = pl.BlockSpec((L, 1), lambda s, h: (s, 0))
    keys = pl.BlockSpec((1, span, 128), lambda s, h: (s, 0, 0))
    lse = pl.BlockSpec((1, 1, L, HEADS), lambda s, h: (s, h, 0, 0))
    return wide, table, starts, keys, lse


def attention(q_lin, cosine, sine, starts, keys, values, hop, deps=()):
    T, width = q_lin.shape
    groups, span, _ = keys.shape
    L = T // groups
    wide, table, start, key, lse = attention_specs(L, span)
    steps = width // (HEADS * 128)
    return call(
        functools.partial(fwd_kernel, heads=HEADS, rb=ROWS, hop=hop),
        "attend",
        (q_lin, cosine, sine, starts, keys, values),
        deps,
        grid=(groups, steps),
        in_specs=[wide, table, table, start, key, key],
        out_specs=[wide, wide, lse],
        out_shape=[
            jax.ShapeDtypeStruct((T, width), bf16),
            jax.ShapeDtypeStruct((T, width), bf16),
            jax.ShapeDtypeStruct((groups, steps, L, HEADS), f32),
        ],
    )


def attention_back(queries, attended, d_attended, lses, cosine, sine, starts, keys, values, hop, deps=()):
    T, width = queries.shape
    groups, span, _ = keys.shape
    L = T // groups
    wide, table, start, key, lse = attention_specs(L, span)
    steps = width // (HEADS * 128)
    return call(
        functools.partial(bwd_kernel, heads=HEADS, rb=ROWS, hop=hop),
        "attend_back",
        (queries, attended, d_attended, lses, cosine, sine, starts, keys, values),
        deps,
        grid=(groups, steps),
        in_specs=[wide, wide, wide, lse, table, table, start, key, key],
        out_specs=[wide, key, key],
        out_shape=[
            jax.ShapeDtypeStruct((T, width), bf16),
            jax.ShapeDtypeStruct((groups, span, 128), f32),
            jax.ShapeDtypeStruct((groups, span, 128), f32),
        ],
    )


def whole(a):
    return pl.BlockSpec(a.shape, lambda *i: (0,) * a.ndim, pipeline_mode=ONCE)


def shape(dims, dtype=bf16):
    return jax.ShapeDtypeStruct(dims, dtype)


def norm_keys(tokens, gain, w_kv, cosine, sine):
    T, D = tokens.shape
    block = 128
    hd = w_kv.shape[1] // 2

    def kernel(x_ref, g_ref, w_ref, c_ref, s_ref, n_ref, inv_ref, kv_ref):
        x = x_ref[...].astype(f32)
        inv = lax.rsqrt(jnp.mean(x * x, axis=1, keepdims=True) + eps)
        normed = (x * inv * g_ref[...]).astype(bf16)
        n_ref[...] = normed
        inv_ref[...] = inv
        kv = dot(normed, w_ref[...], 1, 0)
        kv_ref[:, :hd] = turn(kv[:, :hd], c_ref[...], s_ref[...]).astype(bf16)
        kv_ref[:, hd:] = kv[:, hd:].astype(bf16)

    row = lambda w: pl.BlockSpec((block, w), lambda i: (i, 0))
    return call(
        kernel, "norm_keys", (tokens, gain.reshape(1, D), w_kv, cosine, sine), grid=(T // block,),
        in_specs=[row(D), pl.BlockSpec((1, D), lambda i: (0, 0)), whole(w_kv), row(hd), row(hd)],
        out_specs=[row(D), row(1), row(2 * hd)],
        out_shape=[shape((T, D)), shape((T, 1), f32), shape((T, 2 * hd))],
        vmem=56,
    )


def project_query(normed, w_query, deps=()):
    T, D = normed.shape
    N = w_query.shape[1]
    block = 512

    def kernel(a_ref, b_ref, o_ref):
        o_ref[...] = dot(a_ref[...], b_ref[...], 1, 0)

    return call(
        kernel, "query", (normed, w_query), deps, grid=(N // block,),
        in_specs=[whole(normed), pl.BlockSpec((D, block), lambda i: (0, i))],
        out_specs=pl.BlockSpec((T, block), lambda i: (0, i)),
        out_shape=shape((T, N), f32),
        vmem=56,
    )


def project_out(attended, w_output, x_rows, gain, deps=(), passes=()):
    T, D = x_rows.shape
    block = 512
    steps = D // block

    def kernel(a_ref, w_ref, x_ref, g_ref, mid_ref, n_ref, inv_ref, sq_ref):
        i = pl.program_id(0)
        part = x_ref[...].astype(f32) + dot(a_ref[...], w_ref[...], 1, 0)
        mid_ref[:, pl.ds(i * block, block)] = part
        sq = jnp.sum(part * part, axis=1, keepdims=True)

        @pl.when(i == 0)
        def _():
            sq_ref[...] = sq

        @pl.when(i > 0)
        def _():
            sq_ref[...] += sq

        @pl.when(i == steps - 1)
        def _():
            inv = lax.rsqrt(sq_ref[...] * (1.0 / D) + eps)
            inv_ref[...] = inv
            n_ref[...] = (mid_ref[...] * inv * g_ref[...]).astype(bf16)

    full = lambda w: pl.BlockSpec((T, w), lambda i: (0, 0))
    return call(
        kernel, "project_out", (attended, w_output, x_rows, gain.reshape(1, D)), deps, grid=(steps,),
        in_specs=[whole(attended), pl.BlockSpec((D, block), lambda i: (0, i)), pl.BlockSpec((T, block), lambda i: (0, i)), pl.BlockSpec((1, D), lambda i: (0, 0))],
        out_specs=[full(D), full(D), full(1)],
        out_shape=[shape((T, D), f32), shape((T, D)), shape((T, 1), f32)],
        scratch=[pltpu.VMEM((T, 1), f32)],
        passes=passes,
    )


def of_pieces(pieces, block, order=None, rows=None):
    order = order or range(len(pieces))
    rows = rows or [(0, p.shape[0]) for p in pieces]
    specs = [None] * len(pieces)
    starts, at = [None] * len(pieces), 0
    for k in order:
        first, n = rows[k][0] // block, rows[k][1] // block
        specs[k] = pl.BlockSpec(
            (block, pieces[k].shape[1]),
            lambda i, *s, at=at, first=first, n=n: (first + jnp.clip(i - at, 0, n - 1), 0),
        )
        starts[k] = at
        at += n
    order = list(order)

    def read(refs):
        i = pl.program_id(0)
        value = refs[order[0]][...]
        for k in order[1:]:
            value = jnp.where(i >= starts[k], refs[k][...], value)
        return value

    return specs, read, at


def quarter_columns(w):
    return pl.BlockSpec((w.shape[0], w.shape[1] // GROUP), lambda i, q: (0, q[0]), pipeline_mode=ONCE)


def quarter_rows(w):
    return pl.BlockSpec((w.shape[0] // GROUP, w.shape[1]), lambda i, q: (q[0], 0), pipeline_mode=ONCE)


def down_back(quarter, pieces, w_down, deps=()):
    block = 256
    fq = w_down.shape[0] // GROUP
    n = len(pieces)
    specs, read, steps = of_pieces(pieces, block)

    def kernel(q_ref, *refs):
        refs[n + 1][...] = dot(read(refs[:n]), refs[n][...], 1, 1, bf16)

    return call(
        kernel, "down_back", (*pieces, w_down), deps, (quarter,), grid=(steps,),
        in_specs=specs + [quarter_rows(w_down)],
        out_specs=pl.BlockSpec((block, fq), lambda i, q: (i, 0)),
        out_shape=shape((steps * block, fq)),
        vmem=56,
    )


def feed(quarter, pieces, d_hidden, first, w_gate, w_up, deps=(), passes=()):
    block = 256
    fq = w_gate.shape[1] // GROUP
    n = len(pieces)
    specs, read, steps = of_pieces(pieces, block)
    first = first // block

    def kernel(q_ref, *refs):
        dh_ref, wg_ref, wu_ref, h_ref, dg_ref, du_ref = refs[n:]
        value = read(refs[:n])
        gate = dot(value, wg_ref[...], 1, 0)
        up = dot(value, wu_ref[...], 1, 0)
        dh = dh_ref[...].astype(f32)
        sig = jax.nn.sigmoid(gate)
        silu = gate * sig
        h_ref[...] = (silu * up).astype(bf16)
        dg_ref[...] = (dh * up * (sig + silu * (1.0 - sig))).astype(bf16)
        du_ref[...] = (dh * silu).astype(bf16)

    out = pl.BlockSpec((block, fq), lambda i, q: (i, 0))
    return call(
        kernel, "feed", (*pieces, d_hidden, w_gate, w_up), deps, (quarter,), grid=(steps,),
        in_specs=specs
        + [pl.BlockSpec((block, fq), lambda i, q: (i + first, 0)), quarter_columns(w_gate), quarter_columns(w_up)],
        out_specs=[out] * 3,
        out_shape=[shape((steps * block, fq))] * 3,
        passes=passes,
    )


def partial_away(name, quarter, pairs, weights, cb, deps=()):
    block = 256
    T = pairs[0][0].shape[0] // 2
    D = weights[0].shape[1 - cb]
    specs, reads = [], []
    for pair in pairs:
        s, read, steps = of_pieces(pair, block, rows=[(T, T)] * 2)
        specs += s
        reads.append(read)
    m = len(weights)

    def kernel(q_ref, *refs):
        total = None
        for j in range(m):
            part = dot(reads[j](refs[2 * j : 2 * j + 2]), refs[2 * m + j][...], 1, cb)
            total = part if total is None else total + part
        refs[-1][0] = total.astype(bf16)

    per = T // block
    return call(
        kernel, name, (*[p for g in pairs for p in g], *weights), deps, (quarter,), grid=(steps,),
        in_specs=specs + [quarter_columns(w) if cb else quarter_rows(w) for w in weights],
        out_specs=pl.BlockSpec((1, block, D), lambda i, q: (i // per, i % per, 0)),
        out_shape=shape((2, T, D)),
        vmem=56,
    )


def partial_near(name, quarter, pairs, weights, cb, got, deps=()):
    block = 256
    T = pairs[0][0].shape[0] // 2
    D = weights[0].shape[1 - cb]
    per = T // block
    specs, reads = [], []
    for pair in pairs:
        s, read, steps = of_pieces(pair, block, order=(1, 0), rows=[(0, T)] * 2)
        specs += s
        reads.append(read)
    m = len(weights)

    def kernel(q_ref, *refs):
        got_ref, far_ref, own_ref = refs[3 * m :]
        total = got_ref[0].astype(f32)
        for j in range(m):
            total = total + dot(reads[j](refs[2 * j : 2 * j + 2]), refs[2 * m + j][...], 1, cb)
        i = pl.program_id(0)

        @pl.when(i < per)
        def _():
            far_ref[...] = total.astype(bf16)

        @pl.when(i >= per)
        def _():
            own_ref[...] = total.astype(bf16)

    return call(
        kernel, name, (*[p for g in pairs for p in g], *weights, got), deps, (quarter,), grid=(steps,),
        in_specs=specs
        + [quarter_columns(w) if cb else quarter_rows(w) for w in weights]
        + [pl.BlockSpec((1, block, D), lambda i, q: (1 - i // per, i % per, 0))],
        out_specs=[
            pl.BlockSpec((block, D), lambda i, q: (jnp.minimum(i, per - 1), 0)),
            pl.BlockSpec((block, D), lambda i, q: (jnp.maximum(i - per, 0), 0)),
        ],
        out_shape=[shape((T, D))] * 2,
        vmem=56,
    )


def rows_product(name, n_all, d_a, d_b, half, parts, got=None, deps=()):
    D, fq = n_all[0].shape[1], d_a.shape[1]
    T = n_all[0].shape[0]
    blocks, halves = parts
    block = D // (blocks * halves)
    extra = () if got is None else (got,)

    def kernel(s_ref, n0, n1, n2, n3, a_ref, b_ref, *rest):
        total = dot(n0[...], a_ref[:T], 0, 0) + dot(n1[...], a_ref[T:], 0, 0)
        total = total + dot(n2[...], b_ref[:T], 0, 0) + dot(n3[...], b_ref[T:], 0, 0)
        if extra:
            total = total + rest[0][0].astype(f32)
        rest[-1][0] = total.astype(bf16)

    cut = pl.BlockSpec((T, block), lambda i, s: (0, i * halves + s[0]))
    out = pl.BlockSpec((1, block, fq), lambda i, s: (i, 0, 0))
    return call(
        kernel, name, (*n_all, d_a, d_b, *extra), deps, (half,), grid=(blocks,),
        in_specs=[cut] * 4 + [whole(d_a), whole(d_b)] + [out] * len(extra),
        out_specs=out,
        out_shape=shape((blocks, block, fq)),
        vmem=56,
    )


def columns_product(name, h_a, h_b, c_all, half, halves, got=None, deps=()):
    D, fq = c_all[0].shape[1], h_a.shape[1]
    T = c_all[0].shape[0]
    block = 256
    steps = D // halves // block
    extra = () if got is None else (got,)

    def kernel(s_ref, c0, c1, c2, c3, a_ref, b_ref, *rest):
        total = dot(a_ref[:T], c0[...], 0, 0) + dot(a_ref[T:], c1[...], 0, 0)
        total = total + dot(b_ref[:T], c2[...], 0, 0) + dot(b_ref[T:], c3[...], 0, 0)
        if extra:
            total = total + rest[0][...].astype(f32)
        rest[-1][...] = total.astype(bf16)

    cut = pl.BlockSpec((T, block), lambda i, s: (0, s[0] * steps + i))
    out = pl.BlockSpec((fq, block), lambda i, s: (0, i))
    return call(
        kernel, name, (*c_all, h_a, h_b, *extra), deps, (half,), grid=(steps,),
        in_specs=[cut] * 4 + [whole(h_a), whole(h_b)] + [out] * len(extra),
        out_specs=out,
        out_shape=shape((fq, D // halves)),
        vmem=56,
    )


def token_products(name, rows, near, away, half, got=None, deps=(), passes=()):
    T, M = rows[0].shape
    N = near.shape[1] // 2
    block = 512
    extra = () if got is None else (got,)

    def kernel(s_ref, n0, n1, n2, n3, a_ref, b_ref, *rest):
        total = dot(n0[...], a_ref[:T], 0, 0) + dot(n1[...], a_ref[T:], 0, 0)
        total = total + dot(n2[...], b_ref[:T], 0, 0) + dot(n3[...], b_ref[T:], 0, 0)
        if extra:
            total = total + rest[0][...].astype(f32)
        rest[-1][...] = total.astype(bf16)

    cut = pl.BlockSpec((T, block), lambda i, s: (0, i))
    col = pl.BlockSpec((2 * T, N), lambda i, s: (0, s[0]), pipeline_mode=ONCE)
    out = pl.BlockSpec((block, N), lambda i, s: (i, 0))
    return call(
        kernel, name, (*rows, near, away, *extra), deps, (half,), grid=(M // block,),
        in_specs=[cut] * 4 + [col, col] + [out] * len(extra),
        out_specs=out,
        out_shape=shape((M, N)),
        passes=passes,
    )


def mid_back(own, got, mid, inverse, cot, gain, w_output, deps=()):
    T, D = mid.shape
    C = w_output.shape[0]
    block, rows = 512, 128

    def kernel(o_ref, g_ref, m_ref, i_ref, c_ref, gain_ref, w_ref, b_ref, n_ref, a_ref):
        @pl.when(pl.program_id(0) == 0)
        def _():
            for r in range(T // rows):
                sl = pl.ds(r * rows, rows)
                dn = o_ref[sl].astype(f32) + g_ref[sl].astype(f32)
                m, inv = m_ref[sl], i_ref[sl]
                mi = m * inv
                grad = jnp.sum(dn * mi, axis=0, keepdims=True)
                if r == 0:
                    n_ref[...] = grad
                else:
                    n_ref[...] += grad
                e = dn * gain_ref[...]
                mean = jnp.mean(e * mi, axis=1, keepdims=True)
                b_ref[sl] = (c_ref[sl].astype(f32) + inv * (e - mi * mean)).astype(bf16)

        a_ref[...] = dot(b_ref[...], w_ref[...], 1, 1, bf16)

    full = lambda w: pl.BlockSpec((T, w), lambda i: (0, 0))
    vec = pl.BlockSpec((1, D), lambda i: (0, 0))
    return call(
        kernel, "mid_back", (own, got, mid, inverse, cot, gain.reshape(1, D), w_output), deps, grid=(C // block,),
        in_specs=[whole(own), whole(got), whole(mid), full(1), whole(cot), vec, pl.BlockSpec((block, D), lambda i: (i, 0))],
        out_specs=[full(D), vec, pl.BlockSpec((T, block), lambda i: (0, i))],
        out_shape=[shape((T, D)), shape((1, D), f32), shape((T, C))],
        vmem=56,
    )


def tokens_back(d_query, d_kv, w_query, w_kv, d_branch, tokens, inverse, gain, deps=()):
    T, D = tokens.shape
    block, rows = 512, 128
    steps = D // block

    def kernel(q_ref, kv_ref, wq_ref, wkv_ref, b_ref, x_ref, i_ref, gain_ref, t_ref, n_ref, sum_ref):
        i = pl.program_id(0)
        at = pl.ds(i * block, block)
        inv = i_ref[...]
        dn = dot(q_ref[...], wq_ref[...], 1, 1) + dot(kv_ref[...], wkv_ref[...], 1, 1)
        xi = x_ref[...].astype(f32) * inv
        n_ref[...] = jnp.sum(dn * xi, axis=0, keepdims=True)
        e = dn * gain_ref[...]
        t_ref[:, at] = e
        part = jnp.sum(e * xi, axis=1, keepdims=True)

        @pl.when(i == 0)
        def _():
            sum_ref[...] = part

        @pl.when(i > 0)
        def _():
            sum_ref[...] += part

        @pl.when(i == steps - 1)
        def _():
            for r in range(T // rows):
                sl = pl.ds(r * rows, rows)
                iv = i_ref[sl]
                mean = sum_ref[sl] * (1.0 / D)
                t_ref[sl] = b_ref[sl].astype(f32) + iv * (t_ref[sl] - x_full[0][sl].astype(f32) * iv * mean)

    x_full = [None]

    def outer(q_ref, kv_ref, wq_ref, wkv_ref, b_ref, x_ref, xf_ref, i_ref, gain_ref, t_ref, n_ref, sum_ref):
        x_full[0] = xf_ref
        kernel(q_ref, kv_ref, wq_ref, wkv_ref, b_ref, x_ref, i_ref, gain_ref, t_ref, n_ref, sum_ref)

    full = lambda w: pl.BlockSpec((T, w), lambda i: (0, 0))
    vec = pl.BlockSpec((1, block), lambda i: (0, i))
    return call(
        outer, "tokens_back", (d_query, d_kv, w_query, w_kv, d_branch, tokens, tokens, inverse, gain.reshape(1, D)), deps, grid=(steps,),
        in_specs=[
            whole(d_query), whole(d_kv), pl.BlockSpec((block, w_query.shape[1]), lambda i: (i, 0)),
            pl.BlockSpec((block, w_kv.shape[1]), lambda i: (i, 0)), whole(d_branch),
            pl.BlockSpec((T, block), lambda i: (0, i)), whole(tokens), full(1), vec,
        ],
        out_specs=[full(D), vec],
        out_shape=[shape((T, D), f32), shape((1, D), f32)],
        scratch=[pltpu.VMEM((T, 1), f32)],
        vmem=56,
    )


def final_output(mid, own, got, deps=()):
    T, D = mid.shape
    block = 128

    def kernel(m_ref, a_ref, b_ref, o_ref):
        o_ref[...] = (m_ref[...] + a_ref[...].astype(f32) + b_ref[...].astype(f32)).astype(bf16)

    row = pl.BlockSpec((block, D), lambda i: (i, 0))
    return call(
        kernel, "output", (mid, own, got), deps, grid=(T // block,), in_specs=[row] * 3, out_specs=row,
        out_shape=shape((T, D)), vmem=56,
    )


def shards(
    tokens,
    segments,
    norm1_gain,
    w_query,
    w_key,
    w_value,
    w_output,
    norm2_gain,
    w_gate,
    w_up,
    w_down,
    cotangent,
):
    mv = Moves()
    nz, z, ny, nb = mv.nz, mv.z, mv.ny, mv.nb
    n_dev = nz * nb
    groups, L, D = tokens.shape
    hd = w_key.shape[1]
    FF = w_gate.shape[1]
    T = groups * L
    hops = (WINDOW + L - 1) // L
    hop = hops * L
    fq = FF // GROUP
    core, xb = mv.bit(1), mv.bit(2)
    quarter = mv.b % GROUP
    scalar = lambda v: v.astype(jnp.int32).reshape(1)
    qi, yi, xi = scalar(quarter), scalar(mv.y), scalar(xb)
    paired = ny == 2

    rows = tokens.reshape(T, D)
    cot = cotangent.reshape(T, D)
    others = [mv.shift(segments + 1, "z", range(nz), distance) for distance in range(1, nz)]
    cot1 = mv.flip(cot, 1)
    cot2 = mv.flip(cot, 2)
    every = jnp.concatenate([jnp.where(o == 0, big, o) for o in others] + [segments + 1], axis=1)
    starts = jnp.sum((every[:, None, :] <= segments[:, :, None]).astype(jnp.int32), axis=2)
    index = z * L + jnp.arange(L, dtype=jnp.int32)
    positions = (index[None, :] - starts).astype(f32).reshape(T, 1)
    starts_rel = (starts - z * L + hop).reshape(T, 1)
    half = hd // 2
    freq = jnp.exp(-math.log(rope_base) * jnp.arange(half, dtype=f32) / half)
    angle = positions * freq
    cos_half, sin_half = jnp.cos(angle), jnp.sin(angle)
    cosine = jnp.concatenate([cos_half, cos_half], axis=1)
    sine = jnp.concatenate([-sin_half, sin_half], axis=1)
    w_kv = jnp.concatenate([w_key, w_value], axis=1)

    normed, inv1, kv = norm_keys(rows, norm1_gain, w_kv, cosine, sine)
    kv = kv.reshape(groups, L, 2 * hd)
    earlier = [mv.shift(kv, "z", range(nz), distance) for distance in range(hops, 0, -1)]
    kv_all = jnp.concatenate(earlier + [kv], axis=1)
    keys, values = kv_all[:, :, :hd], kv_all[:, :, hd:]
    q_lin = project_query(normed, w_query, (kv,))
    attended, queries, lses = attention(q_lin, cosine, sine, starts_rel, keys, values, hop)
    mid, normed2, inv2, cot2 = project_out(attended, w_output, rows, norm2_gain, (cot1,), (cot2,))
    cot3 = mv.flip(cot2, 1)

    def of_group(v):
        far = mv.flip(v, GROUP)
        return v, mv.flip(v, 1), far, mv.flip(far, 1)

    normed_all, attended_all = (of_group(normed), of_group(attended)) if paired else ((), ())

    n1 = mv.flip(normed2, 1)
    n2 = mv.flip(normed2, 2)
    d_hidden = down_back(qi, (cot, cot1, cot2, cot3), w_down, (normed2,))
    h_a, dg_a, du_a, n2 = feed(qi, (normed2, n1), d_hidden, 0, w_gate, w_up, normed_all[1:], (n2,))
    n3 = mv.flip(n2, 1)
    h_b, dg_b, du_b = feed(qi, (n2, n3), d_hidden, 2 * T, w_gate, w_up, (du_a,))
    n_all, c_all = (normed2, n1, n2, n3), (cot, cot1, cot2, cot3)
    same_quarter = [[k * GROUP + q for k in range(nz * ny)] for q in range(GROUP)]

    def sum_all(grad):
        return lax.psum_scatter(grad, AXES, scatter_dimension=0, tiled=True, axis_index_groups=same_quarter)

    def send_rows(name, d_a, d_b, deps):
        if not paired:
            return rows_product(name, n_all, d_a, d_b, 0 * yi, (D // 256, 1), None, deps), None
        part = rows_product(name, n_all, d_a, d_b, 1 - yi, (nz, 2), None, deps)
        return part, mv.flip(part, GROUP)

    def keep_rows(name, sent, d_a, d_b, deps):
        if not paired:
            return sent[0], sum_all(sent[0].reshape(D, fq))[None]
        part = rows_product(name, n_all, d_a, d_b, yi, (nz, 2), sent[1], deps)
        return part, lax.psum_scatter(part, "seq", scatter_dimension=0, tiled=True)

    dn_pairs = [[dg_a, dg_b], [du_a, du_b]]
    gate_sent = send_rows("gate_send", dg_a, dg_b, (du_b,) + attended_all[1:])
    dn_away = partial_away("dn2_away", qi, dn_pairs, [w_gate, w_up], 1, (gate_sent[0],))
    dn_got = mv.flip(dn_away, 1)
    out_away = partial_away("out_away", qi, [[h_a, h_b]], [w_down], 0, (dn_away,))
    dn_far, dn_own = partial_near("dn2_near", qi, dn_pairs, [w_gate, w_up], 1, dn_got, (out_away,))
    dn_last = mv.flip(dn_far, 2)
    out_got = mv.flip(out_away, 1)
    up_sent = send_rows("up_send", du_a, du_b, (dn_far,))
    halves = 2 if paired else 1
    first_half = 1 - yi if paired else 0 * yi
    down_sent = columns_product("down_send", h_a, h_b, c_all, first_half, halves, None, (up_sent[0],))
    gate_kept, r_gate = keep_rows("gate_keep", gate_sent, dg_a, dg_b, (down_sent,))
    d_branch, norm2_term, d_attended = mid_back(
        dn_own, dn_last, mid, inv2, cot, norm2_gain, w_output, (gate_kept,)
    )
    out_far, out_own = partial_near("out_near", qi, [[h_a, h_b]], [w_down], 0, out_got, (d_attended,))
    out_last = mv.flip(out_far, 2)
    if paired:
        down_got = mv.flip(down_sent, GROUP)

    def to_quarters(d):
        cut = lambda v, i: lax.dynamic_slice_in_dim(v, i * (v.shape[1] // 2), v.shape[1] // 2, 1)
        chip = jnp.concatenate([cut(d, core), mv.flip(cut(d, 1 - core), 1)], axis=0)
        return cut(chip, mv.y), mv.flip(cut(chip, 1 - mv.y), GROUP)

    d_query, dk_all, dv_all = attention_back(
        queries, attended, d_attended, lses, cosine, sine, starts_rel, keys, values, hop, (out_far,)
    )
    dkv_all = jnp.concatenate([dk_all, dv_all], axis=2)
    backs = [
        mv.shift(dkv_all[:, (hops - k) * L : (hops - k + 1) * L].astype(bf16), "z", range(nz), -k)
        for k in range(1, hops + 1)
    ]
    if paired:
        db_near, db_away = to_quarters(d_branch)
        out_sent = token_products("w_out_send", attended_all, db_near, db_away, 1 - xi, None, (d_query,))
        out_recv = mv.flip(out_sent, 2)
        last = out_sent
    else:
        last = d_query
    up_kept, r_up = keep_rows("up_keep", up_sent, du_a, du_b, (last, r_gate))
    if paired:
        dq_near, dq_away = to_quarters(d_query)
        query_sent = token_products("w_query_send", normed_all, dq_near, dq_away, 1 - xi, None, (up_kept,))
        query_recv = mv.flip(query_sent, 2)
        g_out, *backs = token_products(
            "w_out_keep", attended_all, db_near, db_away, xi, out_recv, (query_sent,), backs
        )
        last = g_out
        r_out = lax.psum_scatter(g_out, "seq", scatter_dimension=0, tiled=True)
    own = dkv_all[:, hop:]
    for back in backs:
        own = own + back.astype(f32)
    own = own.reshape(T, 2 * hd)
    swapped = jnp.concatenate([own[:, half:hd], own[:, :half]], axis=1)
    d_key = (own[:, :hd] * cosine - swapped * sine).astype(bf16)
    d_kv = jnp.concatenate([d_key, own[:, hd:].astype(bf16)], axis=1)

    grad_tokens, norm1_term = tokens_back(
        d_query, d_kv, w_query, w_kv, d_branch, rows, inv1, norm1_gain, (last,)
    )
    output = final_output(mid, out_own, out_last, (norm1_term,))
    g_kv = dot(normed, d_kv, 0, 0, bf16)
    if paired:
        terms = jnp.concatenate([norm1_term, norm2_term, jnp.zeros((126, D), f32)], axis=0).T
        g_kv = jnp.concatenate([g_kv, terms.astype(bf16)], axis=1)
        width = g_kv.shape[1]
        g_kv = g_kv.reshape(nz, 2, 2, 2, D // n_dev, width)
        for axis, mask in ((3, 1), (2, 2), (1, GROUP)):
            bit = mv.bit(mask)
            away = mv.flip(lax.dynamic_index_in_dim(g_kv, 1 - bit, axis, keepdims=False), mask)
            kept = lax.dynamic_index_in_dim(g_kv, bit, axis, keepdims=False)
            g_kv = (kept.astype(f32) + away.astype(f32)).astype(bf16)
        r_kv = lax.psum_scatter(g_kv, "seq", scatter_dimension=0, tiled=True)[0].astype(f32)
        norms = r_kv[:, 2 * hd : 2 * hd + 2].T
    else:
        r_kv = lax.psum_scatter(g_kv, AXES, scatter_dimension=0, tiled=True).astype(f32)
        norms = jnp.concatenate([norm1_term, norm2_term], axis=0)
        norms = norms.reshape(2, n_dev, D // n_dev).transpose(1, 0, 2)
        norms = jnp.sum(lax.all_to_all(norms, AXES, 0, 0, tiled=True), axis=0)

    if paired:
        down_kept = columns_product("down_keep", h_a, h_b, c_all, yi, 2, down_got, (output, r_up))
        r_down = lax.psum_scatter(down_kept, "seq", scatter_dimension=0, tiled=True)
        g_query = token_products("w_query_keep", normed_all, dq_near, dq_away, xi, query_recv, (down_kept, r_out))

        def finish(r):
            r = lax.all_to_all(r.reshape(nb, D // n_dev, D // nb), "batch", 0, 0, tiled=True)
            order = [y_ * GROUP + x_ * 2 + c_ for c_ in range(2) for y_ in range(2) for x_ in range(2)]
            return jnp.concatenate([r[b_] for b_ in order], axis=1).astype(f32)

        r_query = lax.psum_scatter(g_query, "seq", scatter_dimension=0, tiled=True)
        grad_output, grad_query = finish(r_out), finish(r_query)
        r_down = r_down.reshape(2, fq // (2 * nz), D // 2)
        parts = []
        for k in range(2):
            pairs = [
                (z_ * nb + b_, (b_ % GROUP) * ny * nz + z_ * ny + (b_ // GROUP) ^ k)
                for z_ in range(nz)
                for b_ in range(nb)
            ]
            piece = lax.dynamic_index_in_dim(r_down, mv.y ^ k, 0, keepdims=False)
            parts.append(lax.ppermute(piece, AXES, pairs))
        first = jnp.where(core == 0, parts[0], parts[1])
        second = jnp.where(core == 0, parts[1], parts[0])
        grad_down = jnp.concatenate([first, second], axis=1).astype(f32)
    else:
        r_down = sum_all(down_sent)
        pairs = [
            (z_ * nb + b_, (b_ % GROUP) * ny * nz + z_ * ny + b_ // GROUP)
            for z_ in range(nz)
            for b_ in range(nb)
        ]
        grad_down = lax.ppermute(r_down, AXES, pairs).astype(f32)
        every_device = lambda g: lax.psum_scatter(g, AXES, scatter_dimension=0, tiled=True).astype(f32)
        grad_output = every_device(dot(attended, d_branch, 0, 0, bf16))
        grad_query = every_device(dot(normed, d_query, 0, 0, bf16))

    fours = [[k * GROUP + q for q in range(GROUP)] for k in range(ny)]

    def finish_quarter(r):
        k, height, width = r.shape
        r = r.reshape(k, GROUP, height // GROUP, width).transpose(1, 0, 2, 3)
        r = lax.all_to_all(r, "batch", 0, 0, tiled=True, axis_index_groups=fours)
        return r.transpose(1, 2, 0, 3).reshape(k, height // GROUP, FF).astype(f32)

    gu = finish_quarter(jnp.concatenate([r_gate, r_up], axis=0))
    return (
        output.reshape(groups, L, D),
        grad_tokens.reshape(groups, L, D),
        norms[0],
        grad_query,
        r_kv[:, :hd],
        r_kv[:, hd : 2 * hd],
        grad_output,
        norms[1],
        gu[0],
        gu[1],
        grad_down,
    )


def solution(mesh):
    data, vector, rows = P("batch", "seq", None), P(AXES), P(AXES, None)
    return jax.shard_map(
        shards,
        mesh=mesh,
        in_specs=(data, P("batch", "seq")) + (P(),) * 9 + (data,),
        out_specs=(data, data, vector, rows, rows, rows, rows, vector, rows, rows, rows),
        check_vma=False,
    )
```

```python
import functools
import math

import jax
import jax.numpy as jnp
from jax import lax
from jax.experimental import pallas as pl
from jax.experimental.pallas import tpu as pltpu
from jax.sharding import PartitionSpec as P

WINDOW = 512
eps = 1e-05
rope_base = 10000.0
masked = -1e30
big = 1 << 30
AXES = ("seq", "batch")
GROUP = 4
f32 = jnp.float32
bf16 = jnp.bfloat16


MIB = 2**20
ONCE = pl.Buffered(1)
ANY = pl.BlockSpec(memory_space=pl.ANY)
SCALE = 20.0
HOLD_KV = True
COST = dict(
    norm_keys=5, query=9, attend=14, project_out=11, down_back=20, feed=21, gate=19, gate_send=11, up_send=11, down_send=11,
    gate_keep=12, up_keep=12, down_keep=12, dn2_away=20, dn2_near=22, out_away=11, out_near=13, mid_back=14,
    attend_back=23, w_out_send=7, w_out_keep=7, w_query_send=7, w_query_keep=7, tokens_back=14, output=5, hold=1,
)


def call(kernel, name, args, deps=(), scalars=(), grid=(1,), in_specs=(), out_specs=None, out_shape=None, scratch=(), vmem=56, passes=()):
    n_s, n_a, n_d, n_p = len(scalars), len(args), len(deps), len(passes)
    several = isinstance(out_shape, (list, tuple))
    shapes, specs = (list(out_shape), list(out_specs)) if several else ([out_shape], [out_specs])
    n_o = len(shapes)

    def body(*refs):
        at = n_s + n_a + n_d + n_p
        kernel(*refs[: n_s + n_a], *refs[at : at + n_o], *refs[at + n_o + n_p :])

    out = pl.pallas_call(
        body,
        grid_spec=pltpu.PrefetchScalarGridSpec(
            num_scalar_prefetch=n_s,
            grid=grid,
            in_specs=list(in_specs) + [ANY] * (n_d + n_p),
            out_specs=specs + [ANY] * n_p,
            scratch_shapes=list(scratch),
        ),
        out_shape=shapes + [jax.ShapeDtypeStruct(p.shape, p.dtype) for p in passes],
        input_output_aliases={n_s + n_a + n_d + i: n_o + i for i in range(n_p)},
        compiler_params=pltpu.CompilerParams(vmem_limit_bytes=vmem * MIB),
        cost_estimate=pl.CostEstimate(flops=int(SCALE * COST[name] * 10**9), bytes_accessed=1, transcendentals=0),
        name=name,
    )(*scalars, *args, *deps, *passes)
    return out if several or passes else out[0]


def dot(a, b, ca, cb, out=f32):
    return lax.dot_general(a, b, (((ca,), (cb,)), ((), ())), preferred_element_type=f32).astype(out)


class Moves:
    def __init__(self):
        self.nz, self.nb = lax.axis_size("seq"), lax.axis_size("batch")
        self.z, self.b = lax.axis_index("seq"), lax.axis_index("batch")
        self.ny = self.nb // GROUP
        self.y = self.b // GROUP

    def flip(self, value, mask):
        nz, nb = self.nz, self.nb
        pairs = [(z * nb + b, z * nb + (b ^ mask)) for z in range(nz) for b in range(nb)]
        return lax.ppermute(value, AXES, pairs)

    def shift(self, value, axis, sources, step):
        nz, ny, nb = self.nz, self.ny, self.nb
        pairs = []
        for z in range(nz):
            for b in range(nb):
                y, q = b // GROUP, b % GROUP
                at, size = (z, nz) if axis == "z" else (y, ny)
                if at in sources and 0 <= at + step < size:
                    to = (z + step, y) if axis == "z" else (z, y + step)
                    pairs.append((z * nb + b, to[0] * nb + to[1] * GROUP + q))
        return lax.ppermute(value, AXES, pairs)

    def bit(self, mask):
        return (self.b // mask) % 2


def turn(u, cosine, sine):
    return u * cosine + pltpu.roll(u, 64, 1) * sine


def mask_bias(starts, rows, first_row, keys, first_key, hop):
    qi = lax.broadcasted_iota(jnp.int32, (rows, keys), 0) + (first_row + hop)
    kj = lax.broadcasted_iota(jnp.int32, (rows, keys), 1) + first_key
    allow = (kj <= qi) & (qi - kj < WINDOW) & (kj >= starts)
    return jnp.where(allow, 0.0, masked)


def row_blocks(rows, block, hop):
    for r in range(0, rows, block):
        first = max(0, r + hop - WINDOW)
        first -= first % 128
        yield pl.ds(r, block), r, first, r + block + hop - first


def masked_scores(q, k, bias):
    rows, keys = bias.shape
    s = dot(q, k, 1, 1)
    return (s.reshape(s.shape[0] // rows, rows, keys) + bias[None]).reshape(s.shape)


def fwd_kernel(q_ref, cos_ref, sin_ref, start_ref, k_ref, v_ref, o_ref, qr_ref, lse_ref, *, hop):
    scale = math.log2(math.e) / math.sqrt(128)
    for sl, r, first, count in row_blocks(q_ref.shape[0], ROWS, hop):
        bias = mask_bias(start_ref[sl, :], ROWS, r, count, first, hop)
        cosine, sine = cos_ref[sl, :] * scale, sin_ref[sl, :] * scale
        kk, vv = k_ref[0, pl.ds(first, count), :], v_ref[0, pl.ds(first, count), :]
        for g in range(0, HEADS, TOGETHER):
            heads = range(g, g + TOGETHER)
            parts = []
            for h in heads:
                hs = pl.ds(h * 128, 128)
                part = turn(q_ref[sl, hs], cosine, sine).astype(bf16)
                qr_ref[sl, hs] = part
                parts.append(part)
            s = masked_scores(jnp.concatenate(parts, axis=0), kk, bias)
            top = jnp.max(s, axis=1, keepdims=True)
            e = jnp.exp2(s - top)
            total = jnp.sum(e, axis=1, keepdims=True)
            o = dot(e.astype(bf16), vv, 1, 0) * (1.0 / total)
            lse = top + jnp.log2(total)
            for i, h in enumerate(heads):
                at = slice(i * ROWS, (i + 1) * ROWS)
                o_ref[sl, pl.ds(h * 128, 128)] = o[at].astype(bf16)
                lse_ref[0, 0, sl, h : h + 1] = lse[at]


def bwd_kernel(q_ref, o_ref, do_ref, lse_ref, cos_ref, sin_ref, start_ref, k_ref, v_ref, dq_ref, dk_ref, dv_ref, *, hop):
    scale = 1.0 / math.sqrt(128)

    @pl.when(pl.program_id(1) == 0)
    def _():
        dk_ref[...] = jnp.zeros_like(dk_ref)
        dv_ref[...] = jnp.zeros_like(dv_ref)

    for sl, r, first, count in row_blocks(q_ref.shape[0], ROWS, hop):
        ks = pl.ds(first, count)
        bias = mask_bias(start_ref[sl, :], ROWS, r, count, first, hop)
        cosine, sine = cos_ref[sl, :] * scale, sin_ref[sl, :] * scale
        kk, vv = k_ref[0, ks, :], v_ref[0, ks, :]
        dk = dv = None
        for g in range(0, HEADS, TOGETHER):
            heads = range(g, g + TOGETHER)
            of = lambda ref: [ref[sl, pl.ds(h * 128, 128)] for h in heads]
            q, do = jnp.concatenate(of(q_ref), axis=0), jnp.concatenate(of(do_ref), axis=0)
            o = jnp.concatenate(of(o_ref), axis=0)
            lse = jnp.concatenate([lse_ref[0, 0, sl, h : h + 1] for h in heads], axis=0)
            inner = jnp.sum(do.astype(f32) * o.astype(f32), axis=1, keepdims=True)
            p = jnp.exp2(masked_scores(q, kk, bias) - lse)
            ds = (p * (dot(do, vv, 1, 1) - inner)).astype(bf16)
            dq = dot(ds, kk, 1, 0)
            for i, h in enumerate(heads):
                dq_ref[sl, pl.ds(h * 128, 128)] = turn(dq[i * ROWS : (i + 1) * ROWS], cosine, -sine).astype(bf16)
            dk_part, dv_part = dot(ds, q, 0, 0), dot(p.astype(bf16), do, 0, 0)
            dk = dk_part if dk is None else dk + dk_part
            dv = dv_part if dv is None else dv + dv_part
        dk_ref[0, ks, :] += dk * (1.0 / math.log2(math.e))
        dv_ref[0, ks, :] += dv


HEADS = 8
TOGETHER = 4
ROWS = 128


def attention_specs(L, span):
    wide = pl.BlockSpec((L, HEADS * 128), lambda s, h: (s, h))
    table = pl.BlockSpec((L, 128), lambda s, h: (s, 0))
    starts = pl.BlockSpec((L, 1), lambda s, h: (s, 0))
    keys = pl.BlockSpec((1, span, 128), lambda s, h: (s, 0, 0))
    lse = pl.BlockSpec((1, 1, L, HEADS), lambda s, h: (s, h, 0, 0))
    return wide, table, starts, keys, lse


def attention(q_lin, cosine, sine, starts, keys, values, hop, deps=()):
    T, width = q_lin.shape
    groups, span, _ = keys.shape
    L = T // groups
    wide, table, start, key, lse = attention_specs(L, span)
    steps = width // (HEADS * 128)
    return call(
        functools.partial(fwd_kernel, hop=hop),
        "attend",
        (q_lin, cosine, sine, starts, keys, values),
        deps,
        grid=(groups, steps),
        in_specs=[wide, table, table, start, key, key],
        out_specs=[wide, wide, lse],
        out_shape=[
            jax.ShapeDtypeStruct((T, width), bf16),
            jax.ShapeDtypeStruct((T, width), bf16),
            jax.ShapeDtypeStruct((groups, steps, L, HEADS), f32),
        ],
    )


def attention_back(queries, attended, d_attended, lses, cosine, sine, starts, keys, values, hop, deps=()):
    T, width = queries.shape
    groups, span, _ = keys.shape
    L = T // groups
    wide, table, start, key, lse = attention_specs(L, span)
    steps = width // (HEADS * 128)
    return call(
        functools.partial(bwd_kernel, hop=hop),
        "attend_back",
        (queries, attended, d_attended, lses, cosine, sine, starts, keys, values),
        deps,
        grid=(groups, steps),
        in_specs=[wide, wide, wide, lse, table, table, start, key, key],
        out_specs=[wide, key, key],
        out_shape=[
            jax.ShapeDtypeStruct((T, width), bf16),
            jax.ShapeDtypeStruct((groups, span, 128), f32),
            jax.ShapeDtypeStruct((groups, span, 128), f32),
        ],
    )


def whole(a):
    return pl.BlockSpec(a.shape, lambda *i: (0,) * a.ndim, pipeline_mode=ONCE)


def shape(dims, dtype=bf16):
    return jax.ShapeDtypeStruct(dims, dtype)


def hold(value, deps):
    [out] = call(lambda: None, "hold", (), deps, out_shape=[], out_specs=[], passes=(value,))
    return out


def norm_keys(tokens, gain, w_kv, cosine, sine):
    T, D = tokens.shape
    block = 128
    hd = w_kv.shape[1] // 2

    def kernel(x_ref, g_ref, w_ref, c_ref, s_ref, n_ref, inv_ref, kv_ref):
        x = x_ref[...].astype(f32)
        inv = lax.rsqrt(jnp.mean(x * x, axis=1, keepdims=True) + eps)
        normed = (x * inv * g_ref[...]).astype(bf16)
        n_ref[...] = normed
        inv_ref[...] = inv
        kv = dot(normed, w_ref[...], 1, 0)
        kv_ref[:, :hd] = turn(kv[:, :hd], c_ref[...], s_ref[...]).astype(bf16)
        kv_ref[:, hd:] = kv[:, hd:].astype(bf16)

    row = lambda w: pl.BlockSpec((block, w), lambda i: (i, 0))
    return call(
        kernel, "norm_keys", (tokens, gain.reshape(1, D), w_kv, cosine, sine), grid=(T // block,),
        in_specs=[row(D), pl.BlockSpec((1, D), lambda i: (0, 0)), whole(w_kv), row(hd), row(hd)],
        out_specs=[row(D), row(1), row(2 * hd)],
        out_shape=[shape((T, D)), shape((T, 1), f32), shape((T, 2 * hd))],
        vmem=56,
    )


def project_query(normed, w_query, deps=()):
    T, D = normed.shape
    N = w_query.shape[1]
    block = 512

    def kernel(a_ref, b_ref, o_ref):
        o_ref[...] = dot(a_ref[...], b_ref[...], 1, 0)

    return call(
        kernel, "query", (normed, w_query), deps, grid=(N // block,),
        in_specs=[whole(normed), pl.BlockSpec((D, block), lambda i: (0, i))],
        out_specs=pl.BlockSpec((T, block), lambda i: (0, i)),
        out_shape=shape((T, N), f32),
        vmem=56,
    )


def project_out(attended, w_output, x_rows, gain, deps=(), passes=()):
    T, D = x_rows.shape
    block = 512
    steps = D // block

    def kernel(a_ref, w_ref, x_ref, g_ref, mid_ref, n_ref, inv_ref, sq_ref):
        i = pl.program_id(0)
        part = x_ref[...].astype(f32) + dot(a_ref[...], w_ref[...], 1, 0)
        mid_ref[:, pl.ds(i * block, block)] = part
        sq = jnp.sum(part * part, axis=1, keepdims=True)

        @pl.when(i == 0)
        def _():
            sq_ref[...] = sq

        @pl.when(i > 0)
        def _():
            sq_ref[...] += sq

        @pl.when(i == steps - 1)
        def _():
            inv = lax.rsqrt(sq_ref[...] * (1.0 / D) + eps)
            inv_ref[...] = inv
            n_ref[...] = (mid_ref[...] * inv * g_ref[...]).astype(bf16)

    full = lambda w: pl.BlockSpec((T, w), lambda i: (0, 0))
    return call(
        kernel, "project_out", (attended, w_output, x_rows, gain.reshape(1, D)), deps, grid=(steps,),
        in_specs=[whole(attended), pl.BlockSpec((D, block), lambda i: (0, i)), pl.BlockSpec((T, block), lambda i: (0, i)), pl.BlockSpec((1, D), lambda i: (0, 0))],
        out_specs=[full(D), full(D), full(1)],
        out_shape=[shape((T, D), f32), shape((T, D)), shape((T, 1), f32)],
        scratch=[pltpu.VMEM((T, 1), f32)],
        passes=passes,
    )


def of_pieces(pieces, block, order=None, rows=None):
    order = order or range(len(pieces))
    rows = rows or [(0, p.shape[0]) for p in pieces]
    specs = [None] * len(pieces)
    starts, at = [None] * len(pieces), 0
    for k in order:
        first, n = rows[k][0] // block, rows[k][1] // block
        specs[k] = pl.BlockSpec(
            (block, pieces[k].shape[1]),
            lambda i, *s, at=at, first=first, n=n: (first + jnp.clip(i - at, 0, n - 1), 0),
        )
        starts[k] = at
        at += n
    order = list(order)

    def read(refs):
        i = pl.program_id(0)
        value = refs[order[0]][...]
        for k in order[1:]:
            value = jnp.where(i >= starts[k], refs[k][...], value)
        return value

    return specs, read, at


def quarter_columns(w):
    return pl.BlockSpec((w.shape[0], w.shape[1] // GROUP), lambda i, q: (0, q[0]), pipeline_mode=ONCE)


def quarter_rows(w):
    return pl.BlockSpec((w.shape[0] // GROUP, w.shape[1]), lambda i, q: (q[0], 0), pipeline_mode=ONCE)


def down_back(quarter, pieces, w_down, deps=()):
    block = 256
    fq = w_down.shape[0] // GROUP
    n = len(pieces)
    specs, read, steps = of_pieces(pieces, block)

    def kernel(q_ref, *refs):
        refs[n + 1][...] = dot(read(refs[:n]), refs[n][...], 1, 1, bf16)

    return call(
        kernel, "down_back", (*pieces, w_down), deps, (quarter,), grid=(steps,),
        in_specs=specs + [quarter_rows(w_down)],
        out_specs=pl.BlockSpec((block, fq), lambda i, q: (i, 0)),
        out_shape=shape((steps * block, fq)),
        vmem=56,
    )


def feed(quarter, pieces, d_hidden, first, w_gate, w_up, deps=(), passes=()):
    block = 256
    fq = w_gate.shape[1] // GROUP
    n = len(pieces)
    specs, read, steps = of_pieces(pieces, block)
    first = first // block

    def kernel(q_ref, *refs):
        dh_ref, wg_ref, wu_ref, h_ref, dg_ref, du_ref = refs[n:]
        value = read(refs[:n])
        gate = dot(value, wg_ref[...], 1, 0)
        up = dot(value, wu_ref[...], 1, 0)
        dh = dh_ref[...].astype(f32)
        sig = jax.nn.sigmoid(gate)
        silu = gate * sig
        h_ref[...] = (silu * up).astype(bf16)
        dg_ref[...] = (dh * up * (sig + silu * (1.0 - sig))).astype(bf16)
        du_ref[...] = (dh * silu).astype(bf16)

    out = pl.BlockSpec((block, fq), lambda i, q: (i, 0))
    return call(
        kernel, "feed", (*pieces, d_hidden, w_gate, w_up), deps, (quarter,), grid=(steps,),
        in_specs=specs
        + [pl.BlockSpec((block, fq), lambda i, q: (i + first, 0)), quarter_columns(w_gate), quarter_columns(w_up)],
        out_specs=[out] * 3,
        out_shape=[shape((steps * block, fq))] * 3,
        passes=passes,
    )


def partial_away(name, quarter, pairs, weights, cb, deps=()):
    block = 256
    T = pairs[0][0].shape[0] // 2
    D = weights[0].shape[1 - cb]
    specs, reads = [], []
    for pair in pairs:
        s, read, steps = of_pieces(pair, block, rows=[(T, T)] * 2)
        specs += s
        reads.append(read)
    m = len(weights)

    def kernel(q_ref, *refs):
        total = None
        for j in range(m):
            part = dot(reads[j](refs[2 * j : 2 * j + 2]), refs[2 * m + j][...], 1, cb)
            total = part if total is None else total + part
        refs[-1][0] = total.astype(bf16)

    per = T // block
    return call(
        kernel, name, (*[p for g in pairs for p in g], *weights), deps, (quarter,), grid=(steps,),
        in_specs=specs + [quarter_columns(w) if cb else quarter_rows(w) for w in weights],
        out_specs=pl.BlockSpec((1, block, D), lambda i, q: (i // per, i % per, 0)),
        out_shape=shape((2, T, D)),
        vmem=56,
    )


def partial_near(name, quarter, pairs, weights, cb, got, deps=()):
    block = 256
    T = pairs[0][0].shape[0] // 2
    D = weights[0].shape[1 - cb]
    per = T // block
    specs, reads = [], []
    for pair in pairs:
        s, read, steps = of_pieces(pair, block, order=(1, 0), rows=[(0, T)] * 2)
        specs += s
        reads.append(read)
    m = len(weights)

    def kernel(q_ref, *refs):
        got_ref, far_ref, own_ref = refs[3 * m :]
        total = got_ref[0].astype(f32)
        for j in range(m):
            total = total + dot(reads[j](refs[2 * j : 2 * j + 2]), refs[2 * m + j][...], 1, cb)
        i = pl.program_id(0)

        @pl.when(i < per)
        def _():
            far_ref[...] = total.astype(bf16)

        @pl.when(i >= per)
        def _():
            own_ref[...] = total.astype(bf16)

    return call(
        kernel, name, (*[p for g in pairs for p in g], *weights, got), deps, (quarter,), grid=(steps,),
        in_specs=specs
        + [quarter_columns(w) if cb else quarter_rows(w) for w in weights]
        + [pl.BlockSpec((1, block, D), lambda i, q: (1 - i // per, i % per, 0))],
        out_specs=[
            pl.BlockSpec((block, D), lambda i, q: (jnp.minimum(i, per - 1), 0)),
            pl.BlockSpec((block, D), lambda i, q: (jnp.maximum(i - per, 0), 0)),
        ],
        out_shape=[shape((T, D))] * 2,
        vmem=56,
    )


def rows_product(name, n_all, d_a, d_b, half, parts, got=None, deps=()):
    D, fq = n_all[0].shape[1], d_a.shape[1]
    T = n_all[0].shape[0]
    blocks, halves = parts
    block = D // (blocks * halves)
    extra = () if got is None else (got,)

    def kernel(s_ref, n0, n1, n2, n3, a_ref, b_ref, *rest):
        total = dot(n0[...], a_ref[:T], 0, 0) + dot(n1[...], a_ref[T:], 0, 0)
        total = total + dot(n2[...], b_ref[:T], 0, 0) + dot(n3[...], b_ref[T:], 0, 0)
        if extra:
            total = total + rest[0][0].astype(f32)
        rest[-1][0] = total.astype(bf16)

    cut = pl.BlockSpec((T, block), lambda i, s: (0, i * halves + s[0]))
    out = pl.BlockSpec((1, block, fq), lambda i, s: (i, 0, 0))
    return call(
        kernel, name, (*n_all, d_a, d_b, *extra), deps, (half,), grid=(blocks,),
        in_specs=[cut] * 4 + [whole(d_a), whole(d_b)] + [out] * len(extra),
        out_specs=out,
        out_shape=shape((blocks, block, fq)),
        vmem=56,
    )


def columns_product(name, h_a, h_b, c_all, half, halves, got=None, deps=()):
    D, fq = c_all[0].shape[1], h_a.shape[1]
    T = c_all[0].shape[0]
    block = 256
    steps = D // halves // block
    extra = () if got is None else (got,)

    def kernel(s_ref, c0, c1, c2, c3, a_ref, b_ref, *rest):
        total = dot(a_ref[:T], c0[...], 0, 0) + dot(a_ref[T:], c1[...], 0, 0)
        total = total + dot(b_ref[:T], c2[...], 0, 0) + dot(b_ref[T:], c3[...], 0, 0)
        if extra:
            total = total + rest[0][...].astype(f32)
        rest[-1][...] = total.astype(bf16)

    cut = pl.BlockSpec((T, block), lambda i, s: (0, s[0] * steps + i))
    out = pl.BlockSpec((fq, block), lambda i, s: (0, i))
    return call(
        kernel, name, (*c_all, h_a, h_b, *extra), deps, (half,), grid=(steps,),
        in_specs=[cut] * 4 + [whole(h_a), whole(h_b)] + [out] * len(extra),
        out_specs=out,
        out_shape=shape((fq, D // halves)),
        vmem=56,
    )


def token_products(name, rows, d_all, half, got=None, deps=(), passes=()):
    T, M = rows[0].shape
    N = d_all[0].shape[1] // 2
    block = 512
    n = len(rows)
    extra = () if got is None else (got,)

    def kernel(s_ref, *refs):
        total = dot(refs[0][...], refs[n][...], 0, 0)
        for i in range(1, n):
            total = total + dot(refs[i][...], refs[n + i][...], 0, 0)
        if extra:
            total = total + refs[2 * n][...].astype(f32)
        refs[-1][...] = total.astype(bf16)

    cut = pl.BlockSpec((T, block), lambda i, s: (0, i))
    col = pl.BlockSpec((T, N), lambda i, s: (0, s[0]), pipeline_mode=ONCE)
    out = pl.BlockSpec((block, N), lambda i, s: (i, 0))
    return call(
        kernel, name, (*rows, *d_all, *extra), deps, (half,), grid=(M // block,),
        in_specs=[cut] * n + [col] * n + [out] * len(extra),
        out_specs=out,
        out_shape=shape((M, N)),
        passes=passes,
    )


def mid_back(own, got, mid, inverse, cot, gain, w_output, deps=()):
    T, D = mid.shape
    C = w_output.shape[0]
    block, rows = 512, 128

    def kernel(o_ref, g_ref, m_ref, i_ref, c_ref, gain_ref, w_ref, b_ref, n_ref, a_ref):
        @pl.when(pl.program_id(0) == 0)
        def _():
            for r in range(T // rows):
                sl = pl.ds(r * rows, rows)
                dn = o_ref[sl].astype(f32) + g_ref[sl].astype(f32)
                m, inv = m_ref[sl], i_ref[sl]
                mi = m * inv
                grad = jnp.sum(dn * mi, axis=0, keepdims=True)
                if r == 0:
                    n_ref[...] = grad
                else:
                    n_ref[...] += grad
                e = dn * gain_ref[...]
                mean = jnp.mean(e * mi, axis=1, keepdims=True)
                b_ref[sl] = (c_ref[sl].astype(f32) + inv * (e - mi * mean)).astype(bf16)

        a_ref[...] = dot(b_ref[...], w_ref[...], 1, 1, bf16)

    full = lambda w: pl.BlockSpec((T, w), lambda i: (0, 0))
    vec = pl.BlockSpec((1, D), lambda i: (0, 0))
    return call(
        kernel, "mid_back", (own, got, mid, inverse, cot, gain.reshape(1, D), w_output), deps, grid=(C // block,),
        in_specs=[whole(own), whole(got), whole(mid), full(1), whole(cot), vec, pl.BlockSpec((block, D), lambda i: (i, 0))],
        out_specs=[full(D), vec, pl.BlockSpec((T, block), lambda i: (0, i))],
        out_shape=[shape((T, D)), shape((1, D), f32), shape((T, C))],
        vmem=56,
    )


def tokens_back(d_query, d_kv, w_query, w_kv, d_branch, tokens, inverse, gain, deps=()):
    T, D = tokens.shape
    block, rows = 512, 128
    steps = D // block

    def kernel(q_ref, kv_ref, wq_ref, wkv_ref, b_ref, x_ref, i_ref, gain_ref, t_ref, n_ref, sum_ref):
        i = pl.program_id(0)
        at = pl.ds(i * block, block)
        inv = i_ref[...]
        dn = dot(q_ref[...], wq_ref[...], 1, 1) + dot(kv_ref[...], wkv_ref[...], 1, 1)
        xi = x_ref[...].astype(f32) * inv
        n_ref[...] = jnp.sum(dn * xi, axis=0, keepdims=True)
        e = dn * gain_ref[...]
        t_ref[:, at] = e
        part = jnp.sum(e * xi, axis=1, keepdims=True)

        @pl.when(i == 0)
        def _():
            sum_ref[...] = part

        @pl.when(i > 0)
        def _():
            sum_ref[...] += part

        @pl.when(i == steps - 1)
        def _():
            for r in range(T // rows):
                sl = pl.ds(r * rows, rows)
                iv = i_ref[sl]
                mean = sum_ref[sl] * (1.0 / D)
                t_ref[sl] = b_ref[sl].astype(f32) + iv * (t_ref[sl] - x_full[0][sl].astype(f32) * iv * mean)

    x_full = [None]

    def outer(q_ref, kv_ref, wq_ref, wkv_ref, b_ref, x_ref, xf_ref, i_ref, gain_ref, t_ref, n_ref, sum_ref):
        x_full[0] = xf_ref
        kernel(q_ref, kv_ref, wq_ref, wkv_ref, b_ref, x_ref, i_ref, gain_ref, t_ref, n_ref, sum_ref)

    full = lambda w: pl.BlockSpec((T, w), lambda i: (0, 0))
    vec = pl.BlockSpec((1, block), lambda i: (0, i))
    return call(
        outer, "tokens_back", (d_query, d_kv, w_query, w_kv, d_branch, tokens, tokens, inverse, gain.reshape(1, D)), deps, grid=(steps,),
        in_specs=[
            whole(d_query), whole(d_kv), pl.BlockSpec((block, w_query.shape[1]), lambda i: (i, 0)),
            pl.BlockSpec((block, w_kv.shape[1]), lambda i: (i, 0)), whole(d_branch),
            pl.BlockSpec((T, block), lambda i: (0, i)), whole(tokens), full(1), vec,
        ],
        out_specs=[full(D), vec],
        out_shape=[shape((T, D), f32), shape((1, D), f32)],
        scratch=[pltpu.VMEM((T, 1), f32)],
        vmem=56,
    )


def final_output(mid, own, got, deps=()):
    T, D = mid.shape
    block = 128

    def kernel(m_ref, a_ref, b_ref, o_ref):
        o_ref[...] = (m_ref[...] + a_ref[...].astype(f32) + b_ref[...].astype(f32)).astype(bf16)

    row = pl.BlockSpec((block, D), lambda i: (i, 0))
    return call(
        kernel, "output", (mid, own, got), deps, grid=(T // block,), in_specs=[row] * 3, out_specs=row,
        out_shape=shape((T, D)), vmem=56,
    )


def shards(
    tokens,
    segments,
    norm1_gain,
    w_query,
    w_key,
    w_value,
    w_output,
    norm2_gain,
    w_gate,
    w_up,
    w_down,
    cotangent,
):
    mv = Moves()
    nz, z, ny, nb = mv.nz, mv.z, mv.ny, mv.nb
    n_dev = nz * nb
    groups, L, D = tokens.shape
    hd = w_key.shape[1]
    FF = w_gate.shape[1]
    T = groups * L
    hops = (WINDOW + L - 1) // L
    hop = hops * L
    fq = FF // GROUP
    core, xb = mv.bit(1), mv.bit(2)
    quarter = mv.b % GROUP
    scalar = lambda v: v.astype(jnp.int32).reshape(1)
    qi, yi, xi = scalar(quarter), scalar(mv.y), scalar(xb)
    paired = ny == 2

    rows = tokens.reshape(T, D)
    cot = cotangent.reshape(T, D)
    others = [mv.shift(segments + 1, "z", range(nz), distance) for distance in range(1, nz)]
    cot1 = mv.flip(cot, 1)
    cot2 = mv.flip(cot, 2)
    every = jnp.concatenate([jnp.where(o == 0, big, o) for o in others] + [segments + 1], axis=1)
    starts = jnp.sum((every[:, None, :] <= segments[:, :, None]).astype(jnp.int32), axis=2)
    index = z * L + jnp.arange(L, dtype=jnp.int32)
    positions = (index[None, :] - starts).astype(f32).reshape(T, 1)
    starts_rel = (starts - z * L + hop).reshape(T, 1)
    half = hd // 2
    freq = jnp.exp(-math.log(rope_base) * jnp.arange(half, dtype=f32) / half)
    angle = positions * freq
    cos_half, sin_half = jnp.cos(angle), jnp.sin(angle)
    cosine = jnp.concatenate([cos_half, cos_half], axis=1)
    sine = jnp.concatenate([-sin_half, sin_half], axis=1)
    w_kv = jnp.concatenate([w_key, w_value], axis=1)

    normed, inv1, kv = norm_keys(rows, norm1_gain, w_kv, cosine, sine)
    kv = kv.reshape(groups, L, 2 * hd)
    blocks = [kv]
    for _ in range(hops):
        blocks.insert(0, mv.shift(blocks[0], "z", range(nz), 1))
    kv_all = jnp.concatenate(blocks, axis=1)
    keys, values = kv_all[:, :, :hd], kv_all[:, :, hd:]
    q_lin = project_query(normed, w_query, (kv,))
    attended, queries, lses = attention(q_lin, cosine, sine, starts_rel, keys, values, hop)
    mid, normed2, inv2 = project_out(attended, w_output, rows, norm2_gain, (cot1,))
    cot2 = hold(cot2, (normed2,))
    cot3 = mv.flip(cot2, 1)

    def of_group(v):
        far = mv.flip(v, GROUP)
        return v, mv.flip(v, 1), far, mv.flip(far, 1)

    normed_all, attended_all = (of_group(normed), of_group(attended)) if paired else ((), ())

    n1 = mv.flip(normed2, 1)
    n2 = mv.flip(normed2, 2)
    d_hidden = down_back(qi, (cot, cot1, cot2, cot3), w_down, (normed2,))
    h_a, dg_a, du_a = feed(qi, (normed2, n1), d_hidden, 0, w_gate, w_up, normed_all[1:])
    n2 = hold(n2, (du_a,))
    n3 = mv.flip(n2, 1)
    h_b, dg_b, du_b = feed(qi, (n2, n3), d_hidden, 2 * T, w_gate, w_up, (du_a,))
    n_all, c_all = (normed2, n1, n2, n3), (cot, cot1, cot2, cot3)
    same_quarter = [[k * GROUP + q for k in range(nz * ny)] for q in range(GROUP)]

    def sum_all(grad):
        return lax.psum_scatter(grad, AXES, scatter_dimension=0, tiled=True, axis_index_groups=same_quarter)

    def send_rows(name, d_a, d_b, deps):
        if not paired:
            return rows_product(name, n_all, d_a, d_b, 0 * yi, (D // 256, 1), None, deps), None
        part = rows_product(name, n_all, d_a, d_b, 1 - yi, (nz, 2), None, deps)
        return part, mv.flip(part, GROUP)

    def keep_rows(name, sent, d_a, d_b, deps):
        if not paired:
            return sent[0], sum_all(sent[0].reshape(D, fq))[None]
        part = rows_product(name, n_all, d_a, d_b, yi, (nz, 2), sent[1], deps)
        return part, lax.psum_scatter(part, "seq", scatter_dimension=0, tiled=True)

    dn_pairs = [[dg_a, dg_b], [du_a, du_b]]
    halves = 2 if paired else 1
    first_half = 1 - yi if paired else 0 * yi
    up_sent = send_rows("up_send", du_a, du_b, (du_b,) + attended_all[1:])
    g_gate = rows_product("gate", n_all, dg_a, dg_b, 0 * yi, (D // 256, 1), None, (up_sent[0],))
    dg_a = hold(dg_a, (g_gate,))
    dn_pairs = [[dg_a, dg_b], [du_a, du_b]]
    dn_away = partial_away("dn2_away", qi, dn_pairs, [w_gate, w_up], 1, ())
    dn_got = mv.flip(dn_away, 1)
    down_sent = columns_product("down_send", h_a, h_b, c_all, first_half, halves, None, (dn_away,))
    dn_far, dn_own = partial_near("dn2_near", qi, dn_pairs, [w_gate, w_up], 1, dn_got, (down_sent,))
    dn_last = mv.flip(dn_far, 2)
    out_away = partial_away("out_away", qi, [[h_a, h_b]], [w_down], 0, (dn_far,))
    out_got = mv.flip(out_away, 1)
    g_gate = g_gate.reshape(D, fq)
    if paired:
        down_got = mv.flip(down_sent, GROUP)
        z_gate = lax.psum_scatter(g_gate, "seq", scatter_dimension=0, tiled=True)
    else:
        z_gate = sum_all(g_gate)
    up_kept, r_up = keep_rows("up_keep", up_sent, du_a, du_b, (out_away,))
    out_far, out_own = partial_near("out_near", qi, [[h_a, h_b]], [w_down], 0, out_got, (up_kept,))
    out_last = mv.flip(out_far, 2)
    d_branch, norm2_term, d_attended = mid_back(
        dn_own, dn_last, mid, inv2, cot, norm2_gain, w_output, (out_far,)
    )

    def quarters(d):
        w = D // GROUP
        at = core * 2 + mv.y
        return [lax.dynamic_slice_in_dim(d, (at ^ k) * w, w, 1) for k in (0, 2, 1, 3)]

    def exchange(cuts):
        return cuts[0], mv.flip(cuts[1], 1), mv.flip(cuts[2], GROUP), mv.flip(cuts[3], GROUP + 1)

    db_cuts = quarters(d_branch) if paired else ()
    db_all = exchange(db_cuts) if paired else ()
    d_query, dk_all, dv_all = attention_back(
        queries, attended, d_attended, lses, cosine, sine, starts_rel, keys, values, hop, db_cuts
    )
    dkv_all = jnp.concatenate([dk_all, dv_all], axis=2)
    parts = [dkv_all[:, k * L : (k + 1) * L].astype(bf16) for k in range(hops)]
    back = mv.shift(parts[0], "z", range(nz), -1)
    if paired:
        dq_all = exchange(quarters(d_query))
        down_kept = columns_product(
            "down_keep", h_a, h_b, c_all, yi, 2, down_got, (d_query, z_gate) + tuple(db_all[1:2])
        )
        r_down = lax.psum_scatter(down_kept, "seq", scatter_dimension=0, tiled=True)
        last = down_kept
    else:
        r_gate, last = z_gate[None], d_query
    output = final_output(mid, out_own, out_last, (last,))
    last = output
    if paired:
        z_gate = hold(z_gate, (output,)).reshape(2, D // (2 * nz), fq)
        gate_away = mv.flip(lax.dynamic_index_in_dim(z_gate, 1 - mv.y, 0, keepdims=False), GROUP)
    back = hold(back, (last,))
    for part in parts[1:]:
        back = mv.shift((back.astype(f32) + part.astype(f32)).astype(bf16), "z", range(nz), -1)
    if paired:
        out_sent = token_products("w_out_send", attended_all, db_all, 1 - xi, None, (last, r_up) + dq_all[1:])
        out_recv = mv.flip(out_sent, 2)
        query_sent = token_products("w_query_send", normed_all, dq_all, 1 - xi, None, (out_sent,))
        query_recv = mv.flip(query_sent, 2)
        back = hold(back, (query_sent,))
        last = query_sent
    own = dkv_all[:, hop:] + back.astype(f32)
    own = own.reshape(T, 2 * hd)
    swapped = jnp.concatenate([own[:, half:hd], own[:, :half]], axis=1)
    d_key = (own[:, :hd] * cosine - swapped * sine).astype(bf16)
    d_kv = jnp.concatenate([d_key, own[:, hd:].astype(bf16)], axis=1)
    grad_tokens, norm1_term = tokens_back(
        d_query, d_kv, w_query, w_kv, d_branch, rows, inv1, norm1_gain, (last,)
    )
    g_kv = dot(normed, d_kv, 0, 0, bf16)
    if paired:
        terms = jnp.concatenate([norm1_term, norm2_term, jnp.zeros((126, D), f32)], axis=0).T
        size = D // n_dev
        g_kv = jnp.concatenate([g_kv, terms.astype(bf16)], axis=1)
        g_kv = g_kv.reshape(nz, nb, size, 2 * hd + 128).transpose(1, 0, 2, 3)
        g_kv = lax.all_to_all(g_kv, "batch", 0, 0, tiled=True)
        g_out = token_products("w_out_keep", attended_all, db_all, xi, out_recv, (grad_tokens, r_down))
        r_out = lax.psum_scatter(g_out, "seq", scatter_dimension=0, tiled=True)
        g_query = token_products("w_query_keep", normed_all, dq_all, xi, query_recv, (g_out,))
        g_kv = hold(g_kv, (g_query,)) if HOLD_KV else g_kv
        g_kv = jnp.sum(g_kv.astype(f32), axis=0).astype(bf16)
        gate_away = hold(gate_away, (g_out,))
        gate_kept = lax.dynamic_index_in_dim(z_gate, mv.y, 0, keepdims=False)
        r_gate = (gate_kept.astype(f32) + gate_away.astype(f32)).astype(bf16)[None]
        joined = [
            g_query.reshape(nz, D // nz, D // nb),
            g_kv[:, :, : 2 * hd],
            jnp.pad(g_kv[:, :, 2 * hd :], ((0, 0), (0, 0), (0, D // nb - 128))),
        ]
        r_query = lax.psum_scatter(jnp.concatenate(joined, axis=1), "seq", scatter_dimension=0, tiled=True)[0]
        r_kv = r_query[D // nz : D // nz + size].astype(f32)
        norms = r_query[D // nz + size :, :2].astype(f32).T
        r_query = r_query[: D // nz]

        def finish(r):
            r = lax.all_to_all(r.reshape(nb, D // n_dev, D // nb), "batch", 0, 0, tiled=True)
            order = [y_ * GROUP + x_ * 2 + c_ for c_ in range(2) for y_ in range(2) for x_ in range(2)]
            return jnp.concatenate([r[b_] for b_ in order], axis=1).astype(f32)

        grad_output, grad_query = finish(r_out), finish(r_query)
        r_down = r_down.reshape(2, fq // (2 * nz), D // 2)
        parts = []
        for k in range(2):
            pairs = [
                (z_ * nb + b_, (b_ % GROUP) * ny * nz + z_ * ny + (b_ // GROUP) ^ k)
                for z_ in range(nz)
                for b_ in range(nb)
            ]
            piece = lax.dynamic_index_in_dim(r_down, mv.y ^ k, 0, keepdims=False)
            parts.append(lax.ppermute(piece, AXES, pairs))
        first = jnp.where(core == 0, parts[0], parts[1])
        second = jnp.where(core == 0, parts[1], parts[0])
        grad_down = jnp.concatenate([first, second], axis=1).astype(f32)
    else:
        r_kv = lax.psum_scatter(g_kv, AXES, scatter_dimension=0, tiled=True).astype(f32)
        norms = jnp.concatenate([norm1_term, norm2_term], axis=0)
        norms = norms.reshape(2, n_dev, D // n_dev).transpose(1, 0, 2)
        norms = jnp.sum(lax.all_to_all(norms, AXES, 0, 0, tiled=True), axis=0)
        r_down = sum_all(down_sent)
        pairs = [
            (z_ * nb + b_, (b_ % GROUP) * ny * nz + z_ * ny + b_ // GROUP)
            for z_ in range(nz)
            for b_ in range(nb)
        ]
        grad_down = lax.ppermute(r_down, AXES, pairs).astype(f32)
        every_device = lambda g: lax.psum_scatter(g, AXES, scatter_dimension=0, tiled=True).astype(f32)
        grad_output = every_device(dot(attended, d_branch, 0, 0, bf16))
        grad_query = every_device(dot(normed, d_query, 0, 0, bf16))

    fours = [[k * GROUP + q for q in range(GROUP)] for k in range(ny)]

    def finish_quarter(r):
        k, height, width = r.shape
        r = r.reshape(k, GROUP, height // GROUP, width).transpose(1, 0, 2, 3)
        r = lax.all_to_all(r, "batch", 0, 0, tiled=True, axis_index_groups=fours)
        return r.transpose(1, 2, 0, 3).reshape(k, height // GROUP, FF).astype(f32)

    gu = finish_quarter(jnp.concatenate([r_gate, r_up], axis=0))
    return (
        output.reshape(groups, L, D),
        grad_tokens.reshape(groups, L, D),
        norms[0],
        grad_query,
        r_kv[:, :hd],
        r_kv[:, hd:],
        grad_output,
        norms[1],
        gu[0],
        gu[1],
        grad_down,
    )


def solution(mesh):
    data, vector, rows = P("batch", "seq", None), P(AXES), P(AXES, None)
    return jax.shard_map(
        shards,
        mesh=mesh,
        in_specs=(data, P("batch", "seq")) + (P(),) * 9 + (data,),
        out_specs=(data, data, vector, rows, rows, rows, rows, vector, rows, rows, rows),
        check_vma=False,
    )
```

```python
import functools
import math

import jax
import jax.numpy as jnp
from jax import lax
from jax.experimental import pallas as pl
from jax.experimental.pallas import tpu as pltpu
from jax.sharding import PartitionSpec as P

WINDOW = 512
eps = 1e-05
rope_base = 10000.0
masked = -1e30
big = 1 << 30
AXES = ("seq", "batch")
GROUP = 4
f32 = jnp.float32
bf16 = jnp.bfloat16


MIB = 2**20
ONCE = pl.Buffered(1)
ANY = pl.BlockSpec(memory_space=pl.ANY)
SCALE = 20.0
HOLD_KV = True
COST = dict(
    norm_keys=5, query=9, attend=14, project_out=11, down_back=20, feed=21, gate=19, gate_send=11, up_send=11, down_send=11,
    gate_keep=12, up_keep=12, down_keep=12, dn2_away=20, dn2_near=22, out_away=11, out_near=13, mid_back=14,
    attend_back=23, w_out_send=7, w_out_keep=7, w_query_send=7, w_query_keep=7, tokens_back=14, output=5, hold=1, join=1,
)


def call(kernel, name, args, deps=(), scalars=(), grid=(1,), in_specs=(), out_specs=None, out_shape=None, scratch=(), vmem=56, passes=()):
    n_s, n_a, n_d, n_p = len(scalars), len(args), len(deps), len(passes)
    several = isinstance(out_shape, (list, tuple))
    shapes, specs = (list(out_shape), list(out_specs)) if several else ([out_shape], [out_specs])
    n_o = len(shapes)

    def body(*refs):
        at = n_s + n_a + n_d + n_p
        kernel(*refs[: n_s + n_a], *refs[at : at + n_o], *refs[at + n_o + n_p :])

    out = pl.pallas_call(
        body,
        grid_spec=pltpu.PrefetchScalarGridSpec(
            num_scalar_prefetch=n_s,
            grid=grid,
            in_specs=list(in_specs) + [ANY] * (n_d + n_p),
            out_specs=specs + [ANY] * n_p,
            scratch_shapes=list(scratch),
        ),
        out_shape=shapes + [jax.ShapeDtypeStruct(p.shape, p.dtype) for p in passes],
        input_output_aliases={n_s + n_a + n_d + i: n_o + i for i in range(n_p)},
        compiler_params=pltpu.CompilerParams(vmem_limit_bytes=vmem * MIB),
        cost_estimate=pl.CostEstimate(flops=int(SCALE * COST.get(name, 1) * 10**9), bytes_accessed=1, transcendentals=0),
        name=name,
    )(*scalars, *args, *deps, *passes)
    return out if several or passes else out[0]


def dot(a, b, ca, cb, out=f32):
    return lax.dot_general(a, b, (((ca,), (cb,)), ((), ())), preferred_element_type=f32).astype(out)


class Moves:
    def __init__(self):
        self.nz, self.nb = lax.axis_size("seq"), lax.axis_size("batch")
        self.z, self.b = lax.axis_index("seq"), lax.axis_index("batch")
        self.ny = self.nb // GROUP
        self.y = self.b // GROUP

    def flip(self, value, mask):
        nz, nb = self.nz, self.nb
        pairs = [(z * nb + b, z * nb + (b ^ mask)) for z in range(nz) for b in range(nb)]
        return lax.ppermute(value, AXES, pairs)

    def shift(self, value, axis, sources, step):
        nz, ny, nb = self.nz, self.ny, self.nb
        pairs = []
        for z in range(nz):
            for b in range(nb):
                y, q = b // GROUP, b % GROUP
                at, size = (z, nz) if axis == "z" else (y, ny)
                if at in sources and 0 <= at + step < size:
                    to = (z + step, y) if axis == "z" else (z, y + step)
                    pairs.append((z * nb + b, to[0] * nb + to[1] * GROUP + q))
        return lax.ppermute(value, AXES, pairs)

    def bit(self, mask):
        return (self.b // mask) % 2


def turn(u, cosine, sine):
    return u * cosine + pltpu.roll(u, 64, 1) * sine


def mask_bias(starts, rows, first_row, keys, first_key, hop):
    qi = lax.broadcasted_iota(jnp.int32, (rows, keys), 0) + (first_row + hop)
    kj = lax.broadcasted_iota(jnp.int32, (rows, keys), 1) + first_key
    allow = (kj <= qi) & (qi - kj < WINDOW) & (kj >= starts)
    return jnp.where(allow, 0.0, masked)


def row_blocks(rows, block, hop):
    for r in range(0, rows, block):
        first = max(0, r + hop - WINDOW)
        first -= first % 128
        yield pl.ds(r, block), r, first, r + block + hop - first


def masked_scores(q, k, bias):
    rows, keys = bias.shape
    s = dot(q, k, 1, 1)
    return (s.reshape(s.shape[0] // rows, rows, keys) + bias[None]).reshape(s.shape)


def fwd_kernel(q_ref, cos_ref, sin_ref, start_ref, k_ref, v_ref, o_ref, qr_ref, lse_ref, *, hop):
    scale = math.log2(math.e) / math.sqrt(128)
    for sl, r, first, count in row_blocks(q_ref.shape[0], ROWS, hop):
        bias = mask_bias(start_ref[sl, :], ROWS, r, count, first, hop)
        cosine, sine = cos_ref[sl, :] * scale, sin_ref[sl, :] * scale
        kk, vv = k_ref[0, pl.ds(first, count), :], v_ref[0, pl.ds(first, count), :]
        for g in range(0, HEADS, TOGETHER):
            heads = range(g, g + TOGETHER)
            parts = []
            for h in heads:
                hs = pl.ds(h * 128, 128)
                part = turn(q_ref[sl, hs], cosine, sine).astype(bf16)
                qr_ref[sl, hs] = part
                parts.append(part)
            s = masked_scores(jnp.concatenate(parts, axis=0), kk, bias)
            top = jnp.max(s, axis=1, keepdims=True)
            e = jnp.exp2(s - top)
            total = jnp.sum(e, axis=1, keepdims=True)
            o = dot(e.astype(bf16), vv, 1, 0) * (1.0 / total)
            lse = top + jnp.log2(total)
            for i, h in enumerate(heads):
                at = slice(i * ROWS, (i + 1) * ROWS)
                o_ref[sl, pl.ds(h * 128, 128)] = o[at].astype(bf16)
                lse_ref[0, 0, sl, h : h + 1] = lse[at]


def bwd_kernel(q_ref, o_ref, do_ref, lse_ref, cos_ref, sin_ref, start_ref, k_ref, v_ref, dq_ref, dkv_ref, *, hop):
    scale = 1.0 / math.sqrt(128)

    @pl.when(pl.program_id(1) == 0)
    def _():
        dkv_ref[...] = jnp.zeros_like(dkv_ref)

    for sl, r, first, count in row_blocks(q_ref.shape[0], ROWS, hop):
        ks = pl.ds(first, count)
        bias = mask_bias(start_ref[sl, :], ROWS, r, count, first, hop)
        cosine, sine = cos_ref[sl, :] * scale, sin_ref[sl, :] * scale
        kk, vv = k_ref[0, ks, :], v_ref[0, ks, :]
        dk = dv = None
        for g in range(0, HEADS, TOGETHER):
            heads = range(g, g + TOGETHER)
            of = lambda ref: [ref[sl, pl.ds(h * 128, 128)] for h in heads]
            q, do = jnp.concatenate(of(q_ref), axis=0), jnp.concatenate(of(do_ref), axis=0)
            o = jnp.concatenate(of(o_ref), axis=0)
            lse = jnp.concatenate([lse_ref[0, 0, sl, h : h + 1] for h in heads], axis=0)
            inner = jnp.sum(do.astype(f32) * o.astype(f32), axis=1, keepdims=True)
            p = jnp.exp2(masked_scores(q, kk, bias) - lse)
            ds = (p * (dot(do, vv, 1, 1) - inner)).astype(bf16)
            dq = dot(ds, kk, 1, 0)
            for i, h in enumerate(heads):
                dq_ref[sl, pl.ds(h * 128, 128)] = turn(dq[i * ROWS : (i + 1) * ROWS], cosine, -sine).astype(bf16)
            dk_part, dv_part = dot(ds, q, 0, 0), dot(p.astype(bf16), do, 0, 0)
            dk = dk_part if dk is None else dk + dk_part
            dv = dv_part if dv is None else dv + dv_part
        dkv_ref[0, ks, :128] += dk * (1.0 / math.log2(math.e))
        dkv_ref[0, ks, 128:] += dv


HEADS = 8
TOGETHER = 4
ROWS = 128


def attention_specs(L, span):
    wide = pl.BlockSpec((L, HEADS * 128), lambda s, h: (s, h))
    table = pl.BlockSpec((L, 128), lambda s, h: (s, 0))
    starts = pl.BlockSpec((L, 1), lambda s, h: (s, 0))
    keys = pl.BlockSpec((1, span, 128), lambda s, h: (s, 0, 0)), pl.BlockSpec((1, span, 128), lambda s, h: (s, 0, 1))
    lse = pl.BlockSpec((1, 1, L, HEADS), lambda s, h: (s, h, 0, 0))
    return wide, table, starts, keys, lse


def attention(q_lin, cosine, sine, starts, kv, hop, deps=()):
    T, width = q_lin.shape
    groups, span, _ = kv.shape
    L = T // groups
    wide, table, start, key, lse = attention_specs(L, span)
    steps = width // (HEADS * 128)
    return call(
        functools.partial(fwd_kernel, hop=hop),
        "attend",
        (q_lin, cosine, sine, starts, kv, kv),
        deps,
        grid=(groups, steps),
        in_specs=[wide, table, table, start, *key],
        out_specs=[wide, wide, lse],
        out_shape=[
            jax.ShapeDtypeStruct((T, width), bf16),
            jax.ShapeDtypeStruct((T, width), bf16),
            jax.ShapeDtypeStruct((groups, steps, L, HEADS), f32),
        ],
    )


def attention_back(queries, attended, d_attended, lses, cosine, sine, starts, kv, hop, deps=()):
    T, width = queries.shape
    groups, span, _ = kv.shape
    L = T // groups
    wide, table, start, key, lse = attention_specs(L, span)
    steps = width // (HEADS * 128)
    return call(
        functools.partial(bwd_kernel, hop=hop),
        "attend_back",
        (queries, attended, d_attended, lses, cosine, sine, starts, kv, kv),
        deps,
        grid=(groups, steps),
        in_specs=[wide, wide, wide, lse, table, table, start, *key],
        out_specs=[wide, pl.BlockSpec((1, span, 256), lambda s, h: (s, 0, 0))],
        out_shape=[
            jax.ShapeDtypeStruct((T, width), bf16),
            jax.ShapeDtypeStruct((groups, span, 256), f32),
        ],
    )


def whole(a):
    return pl.BlockSpec(a.shape, lambda *i: (0,) * a.ndim, pipeline_mode=ONCE)


def shape(dims, dtype=bf16):
    return jax.ShapeDtypeStruct(dims, dtype)


def hold(value, deps):
    [out] = call(lambda: None, "hold", (), deps, out_shape=[], out_specs=[], passes=(value,))
    return out


def norm_keys(tokens, gain, w_key, w_value, cosine, sine):
    T, D = tokens.shape
    block = 128
    hd = w_key.shape[1]

    def kernel(x_ref, g_ref, wk_ref, wv_ref, c_ref, s_ref, n_ref, inv_ref, kv_ref):
        x = x_ref[...].astype(f32)
        inv = lax.rsqrt(jnp.mean(x * x, axis=1, keepdims=True) + eps)
        normed = (x * inv * g_ref[...]).astype(bf16)
        n_ref[...] = normed
        inv_ref[...] = inv
        kv_ref[:, :hd] = turn(dot(normed, wk_ref[...], 1, 0), c_ref[...], s_ref[...]).astype(bf16)
        kv_ref[:, hd:] = dot(normed, wv_ref[...], 1, 0, bf16)

    row = lambda w: pl.BlockSpec((block, w), lambda i: (i, 0))
    return call(
        kernel, "norm_keys", (tokens, gain.reshape(1, D), w_key, w_value, cosine, sine), grid=(T // block,),
        in_specs=[row(D), pl.BlockSpec((1, D), lambda i: (0, 0)), whole(w_key), whole(w_value), row(hd), row(hd)],
        out_specs=[row(D), row(1), row(2 * hd)],
        out_shape=[shape((T, D)), shape((T, 1), f32), shape((T, 2 * hd))],
        vmem=56,
    )


def project_query(normed, w_query, deps=()):
    T, D = normed.shape
    N = w_query.shape[1]
    block = 512

    def kernel(a_ref, b_ref, o_ref):
        o_ref[...] = dot(a_ref[...], b_ref[...], 1, 0)

    return call(
        kernel, "query", (normed, w_query), deps, grid=(N // block,),
        in_specs=[whole(normed), pl.BlockSpec((D, block), lambda i: (0, i))],
        out_specs=pl.BlockSpec((T, block), lambda i: (0, i)),
        out_shape=shape((T, N), f32),
        vmem=56,
    )


def project_out(attended, w_output, x_rows, gain, deps=(), passes=()):
    T, D = x_rows.shape
    block = 512
    steps = D // block

    def kernel(a_ref, w_ref, x_ref, g_ref, mid_ref, n_ref, inv_ref, sq_ref):
        i = pl.program_id(0)
        part = x_ref[...].astype(f32) + dot(a_ref[...], w_ref[...], 1, 0)
        mid_ref[:, pl.ds(i * block, block)] = part
        sq = jnp.sum(part * part, axis=1, keepdims=True)

        @pl.when(i == 0)
        def _():
            sq_ref[...] = sq

        @pl.when(i > 0)
        def _():
            sq_ref[...] += sq

        @pl.when(i == steps - 1)
        def _():
            inv = lax.rsqrt(sq_ref[...] * (1.0 / D) + eps)
            inv_ref[...] = inv
            n_ref[...] = (mid_ref[...] * inv * g_ref[...]).astype(bf16)

    full = lambda w: pl.BlockSpec((T, w), lambda i: (0, 0))
    return call(
        kernel, "project_out", (attended, w_output, x_rows, gain.reshape(1, D)), deps, grid=(steps,),
        in_specs=[whole(attended), pl.BlockSpec((D, block), lambda i: (0, i)), pl.BlockSpec((T, block), lambda i: (0, i)), pl.BlockSpec((1, D), lambda i: (0, 0))],
        out_specs=[full(D), full(D), full(1)],
        out_shape=[shape((T, D), f32), shape((T, D)), shape((T, 1), f32)],
        scratch=[pltpu.VMEM((T, 1), f32)],
        passes=passes,
    )


def of_pieces(pieces, block, order=None, rows=None):
    order = order or range(len(pieces))
    rows = rows or [(0, p.shape[0]) for p in pieces]
    specs = [None] * len(pieces)
    starts, at = [None] * len(pieces), 0
    for k in order:
        first, n = rows[k][0] // block, rows[k][1] // block
        specs[k] = pl.BlockSpec(
            (block, pieces[k].shape[1]),
            lambda i, *s, at=at, first=first, n=n: (first + jnp.clip(i - at, 0, n - 1), 0),
        )
        starts[k] = at
        at += n
    order = list(order)

    def read(refs):
        i = pl.program_id(0)
        value = refs[order[0]][...]
        for k in order[1:]:
            value = jnp.where(i >= starts[k], refs[k][...], value)
        return value

    return specs, read, at


def quarter_columns(w):
    return pl.BlockSpec((w.shape[0], w.shape[1] // GROUP), lambda i, q: (0, q[0]), pipeline_mode=ONCE)


def quarter_rows(w):
    return pl.BlockSpec((w.shape[0] // GROUP, w.shape[1]), lambda i, q: (q[0], 0), pipeline_mode=ONCE)


def down_back(quarter, pieces, w_down, deps=()):
    block = 256
    fq = w_down.shape[0] // GROUP
    n = len(pieces)
    specs, read, steps = of_pieces(pieces, block)

    def kernel(q_ref, *refs):
        refs[n + 1][...] = dot(read(refs[:n]), refs[n][...], 1, 1, bf16)

    return call(
        kernel, "down_back", (*pieces, w_down), deps, (quarter,), grid=(steps,),
        in_specs=specs + [quarter_rows(w_down)],
        out_specs=pl.BlockSpec((block, fq), lambda i, q: (i, 0)),
        out_shape=shape((steps * block, fq)),
        vmem=56,
    )


def feed(quarter, pieces, d_hidden, first, w_gate, w_up, deps=(), passes=()):
    block = 256
    fq = w_gate.shape[1] // GROUP
    n = len(pieces)
    specs, read, steps = of_pieces(pieces, block)
    first = first // block

    def kernel(q_ref, *refs):
        dh_ref, wg_ref, wu_ref, h_ref, dg_ref, du_ref = refs[n:]
        value = read(refs[:n])
        gate = dot(value, wg_ref[...], 1, 0)
        up = dot(value, wu_ref[...], 1, 0)
        dh = dh_ref[...].astype(f32)
        sig = jax.nn.sigmoid(gate)
        silu = gate * sig
        h_ref[...] = (silu * up).astype(bf16)
        dg_ref[...] = (dh * up * (sig + silu * (1.0 - sig))).astype(bf16)
        du_ref[...] = (dh * silu).astype(bf16)

    out = pl.BlockSpec((block, fq), lambda i, q: (i, 0))
    return call(
        kernel, "feed", (*pieces, d_hidden, w_gate, w_up), deps, (quarter,), grid=(steps,),
        in_specs=specs
        + [pl.BlockSpec((block, fq), lambda i, q: (i + first, 0)), quarter_columns(w_gate), quarter_columns(w_up)],
        out_specs=[out] * 3,
        out_shape=[shape((steps * block, fq))] * 3,
        passes=passes,
    )


def partial_away(name, quarter, pairs, weights, cb, deps=()):
    block = 256
    T = pairs[0][0].shape[0] // 2
    D = weights[0].shape[1 - cb]
    specs, reads = [], []
    for pair in pairs:
        s, read, steps = of_pieces(pair, block, rows=[(T, T)] * 2)
        specs += s
        reads.append(read)
    m = len(weights)

    def kernel(q_ref, *refs):
        total = None
        for j in range(m):
            part = dot(reads[j](refs[2 * j : 2 * j + 2]), refs[2 * m + j][...], 1, cb)
            total = part if total is None else total + part
        refs[-1][0] = total.astype(bf16)

    per = T // block
    return call(
        kernel, name, (*[p for g in pairs for p in g], *weights), deps, (quarter,), grid=(steps,),
        in_specs=specs + [quarter_columns(w) if cb else quarter_rows(w) for w in weights],
        out_specs=pl.BlockSpec((1, block, D), lambda i, q: (i // per, i % per, 0)),
        out_shape=shape((2, T, D)),
        vmem=56,
    )


def partial_near(name, quarter, pairs, weights, cb, got, deps=()):
    block = 256
    T = pairs[0][0].shape[0] // 2
    D = weights[0].shape[1 - cb]
    per = T // block
    specs, reads = [], []
    for pair in pairs:
        s, read, steps = of_pieces(pair, block, order=(1, 0), rows=[(0, T)] * 2)
        specs += s
        reads.append(read)
    m = len(weights)

    def kernel(q_ref, *refs):
        got_ref, far_ref, own_ref = refs[3 * m :]
        total = got_ref[0].astype(f32)
        for j in range(m):
            total = total + dot(reads[j](refs[2 * j : 2 * j + 2]), refs[2 * m + j][...], 1, cb)
        i = pl.program_id(0)

        @pl.when(i < per)
        def _():
            far_ref[...] = total.astype(bf16)

        @pl.when(i >= per)
        def _():
            own_ref[...] = total.astype(bf16)

    return call(
        kernel, name, (*[p for g in pairs for p in g], *weights, got), deps, (quarter,), grid=(steps,),
        in_specs=specs
        + [quarter_columns(w) if cb else quarter_rows(w) for w in weights]
        + [pl.BlockSpec((1, block, D), lambda i, q: (1 - i // per, i % per, 0))],
        out_specs=[
            pl.BlockSpec((block, D), lambda i, q: (jnp.minimum(i, per - 1), 0)),
            pl.BlockSpec((block, D), lambda i, q: (jnp.maximum(i - per, 0), 0)),
        ],
        out_shape=[shape((T, D))] * 2,
        vmem=56,
    )


def rows_product(name, n_all, d_a, d_b, half, parts, got=None, deps=()):
    D, fq = n_all[0].shape[1], d_a.shape[1]
    T = n_all[0].shape[0]
    blocks, halves = parts
    block = D // (blocks * halves)
    extra = () if got is None else (got,)

    def kernel(s_ref, n0, n1, n2, n3, a_ref, b_ref, *rest):
        total = dot(n0[...], a_ref[:T], 0, 0) + dot(n1[...], a_ref[T:], 0, 0)
        total = total + dot(n2[...], b_ref[:T], 0, 0) + dot(n3[...], b_ref[T:], 0, 0)
        if extra:
            total = total + rest[0][0].astype(f32)
        rest[-1][0] = total.astype(bf16)

    cut = pl.BlockSpec((T, block), lambda i, s: (0, i * halves + s[0]))
    out = pl.BlockSpec((1, block, fq), lambda i, s: (i, 0, 0))
    return call(
        kernel, name, (*n_all, d_a, d_b, *extra), deps, (half,), grid=(blocks,),
        in_specs=[cut] * 4 + [whole(d_a), whole(d_b)] + [out] * len(extra),
        out_specs=out,
        out_shape=shape((blocks, block, fq)),
        vmem=56,
    )


def columns_product(name, h_a, h_b, c_all, half, halves, got=None, deps=()):
    D, fq = c_all[0].shape[1], h_a.shape[1]
    T = c_all[0].shape[0]
    block = 256
    steps = D // halves // block
    extra = () if got is None else (got,)

    def kernel(s_ref, c0, c1, c2, c3, a_ref, b_ref, *rest):
        total = dot(a_ref[:T], c0[...], 0, 0) + dot(a_ref[T:], c1[...], 0, 0)
        total = total + dot(b_ref[:T], c2[...], 0, 0) + dot(b_ref[T:], c3[...], 0, 0)
        if extra:
            total = total + rest[0][...].astype(f32)
        rest[-1][...] = total.astype(bf16)

    cut = pl.BlockSpec((T, block), lambda i, s: (0, s[0] * steps + i))
    out = pl.BlockSpec((fq, block), lambda i, s: (0, i))
    return call(
        kernel, name, (*c_all, h_a, h_b, *extra), deps, (half,), grid=(steps,),
        in_specs=[cut] * 4 + [whole(h_a), whole(h_b)] + [out] * len(extra),
        out_specs=out,
        out_shape=shape((fq, D // halves)),
        vmem=56,
    )


def token_products(name, rows, d_all, half, got=None, deps=(), passes=()):
    T, M = rows[0].shape
    N = d_all[0].shape[1] // 2
    block = 512
    n = len(rows)
    extra = () if got is None else (got,)

    def kernel(s_ref, *refs):
        total = dot(refs[0][...], refs[n][...], 0, 0)
        for i in range(1, n):
            total = total + dot(refs[i][...], refs[n + i][...], 0, 0)
        if extra:
            total = total + refs[2 * n][...].astype(f32)
        refs[-1][...] = total.astype(bf16)

    cut = pl.BlockSpec((T, block), lambda i, s: (0, i))
    col = pl.BlockSpec((T, N), lambda i, s: (0, s[0]), pipeline_mode=ONCE)
    out = pl.BlockSpec((block, N), lambda i, s: (i, 0))
    return call(
        kernel, name, (*rows, *d_all, *extra), deps, (half,), grid=(M // block,),
        in_specs=[cut] * n + [col] * n + [out] * len(extra),
        out_specs=out,
        out_shape=shape((M, N)),
        passes=passes,
    )


def mid_back(own, got, mid, inverse, cot, gain, w_output, deps=()):
    T, D = mid.shape
    C = w_output.shape[0]
    block, rows = 512, 128

    def kernel(o_ref, g_ref, m_ref, i_ref, c_ref, gain_ref, w_ref, b_ref, n_ref, a_ref):
        @pl.when(pl.program_id(0) == 0)
        def _():
            for r in range(T // rows):
                sl = pl.ds(r * rows, rows)
                dn = o_ref[sl].astype(f32) + g_ref[sl].astype(f32)
                m, inv = m_ref[sl], i_ref[sl]
                mi = m * inv
                grad = jnp.sum(dn * mi, axis=0, keepdims=True)
                if r == 0:
                    n_ref[...] = grad
                else:
                    n_ref[...] += grad
                e = dn * gain_ref[...]
                mean = jnp.mean(e * mi, axis=1, keepdims=True)
                b_ref[sl] = (c_ref[sl].astype(f32) + inv * (e - mi * mean)).astype(bf16)

        a_ref[...] = dot(b_ref[...], w_ref[...], 1, 1, bf16)

    full = lambda w: pl.BlockSpec((T, w), lambda i: (0, 0))
    vec = pl.BlockSpec((1, D), lambda i: (0, 0))
    return call(
        kernel, "mid_back", (own, got, mid, inverse, cot, gain.reshape(1, D), w_output), deps, grid=(C // block,),
        in_specs=[whole(own), whole(got), whole(mid), full(1), whole(cot), vec, pl.BlockSpec((block, D), lambda i: (i, 0))],
        out_specs=[full(D), vec, pl.BlockSpec((T, block), lambda i: (0, i))],
        out_shape=[shape((T, D)), shape((1, D), f32), shape((T, C))],
        vmem=56,
    )


def tokens_back(d_query, d_kv, w_query, w_key, w_value, d_branch, tokens, inverse, gain, deps=()):
    T, D = tokens.shape
    block, rows = 512, 128
    hd = w_key.shape[1]
    steps = D // block

    def kernel(q_ref, kv_ref, wq_ref, wk_ref, wv_ref, b_ref, x_ref, i_ref, gain_ref, t_ref, n_ref, sum_ref):
        i = pl.program_id(0)
        at = pl.ds(i * block, block)
        inv = i_ref[...]
        dn = dot(q_ref[...], wq_ref[...], 1, 1)
        dn = dn + dot(kv_ref[:, :hd], wk_ref[...], 1, 1) + dot(kv_ref[:, hd:], wv_ref[...], 1, 1)
        xi = x_ref[...].astype(f32) * inv
        n_ref[...] = jnp.sum(dn * xi, axis=0, keepdims=True)
        e = dn * gain_ref[...]
        t_ref[:, at] = e
        part = jnp.sum(e * xi, axis=1, keepdims=True)

        @pl.when(i == 0)
        def _():
            sum_ref[...] = part

        @pl.when(i > 0)
        def _():
            sum_ref[...] += part

        @pl.when(i == steps - 1)
        def _():
            for r in range(T // rows):
                sl = pl.ds(r * rows, rows)
                iv = i_ref[sl]
                mean = sum_ref[sl] * (1.0 / D)
                t_ref[sl] = b_ref[sl].astype(f32) + iv * (t_ref[sl] - x_full[0][sl].astype(f32) * iv * mean)

    x_full = [None]

    def outer(q_ref, kv_ref, wq_ref, wk_ref, wv_ref, b_ref, x_ref, xf_ref, i_ref, gain_ref, t_ref, n_ref, sum_ref):
        x_full[0] = xf_ref
        kernel(q_ref, kv_ref, wq_ref, wk_ref, wv_ref, b_ref, x_ref, i_ref, gain_ref, t_ref, n_ref, sum_ref)

    full = lambda w: pl.BlockSpec((T, w), lambda i: (0, 0))
    vec = pl.BlockSpec((1, block), lambda i: (0, i))
    return call(
        outer, "tokens_back", (d_query, d_kv, w_query, w_key, w_value, d_branch, tokens, tokens, inverse, gain.reshape(1, D)), deps, grid=(steps,),
        in_specs=[
            whole(d_query), whole(d_kv), pl.BlockSpec((block, w_query.shape[1]), lambda i: (i, 0)),
            pl.BlockSpec((block, hd), lambda i: (i, 0)), pl.BlockSpec((block, hd), lambda i: (i, 0)), whole(d_branch),
            pl.BlockSpec((T, block), lambda i: (0, i)), whole(tokens), full(1), vec,
        ],
        out_specs=[full(D), vec],
        out_shape=[shape((T, D), f32), shape((1, D), f32)],
        scratch=[pltpu.VMEM((T, 1), f32)],
        vmem=56,
    )


def final_output(mid, own, got, deps=()):
    T, D = mid.shape
    block = 128

    def kernel(m_ref, a_ref, b_ref, o_ref):
        o_ref[...] = (m_ref[...] + a_ref[...].astype(f32) + b_ref[...].astype(f32)).astype(bf16)

    row = pl.BlockSpec((block, D), lambda i: (i, 0))
    return call(
        kernel, "output", (mid, own, got), deps, grid=(T // block,), in_specs=[row] * 3, out_specs=row,
        out_shape=shape((T, D)), vmem=56,
    )


def join_columns(name, parts, order):
    n, r, w = parts.shape

    def kernel(p_ref, o_ref):
        for k, b in enumerate(order):
            o_ref[:, k * w : (k + 1) * w] = p_ref[b].astype(f32)

    full = lambda d: pl.BlockSpec(d, lambda i: (0,) * len(d))
    return call(kernel, name, (parts,), in_specs=[full(parts.shape)], out_specs=full((r, n * w)), out_shape=shape((r, n * w), f32))


def join_two(name, parts, order):
    n, _, r, w = parts.shape

    def kernel(p_ref, a_ref, b_ref):
        for k, at in enumerate(order):
            a_ref[:, at * w : (at + 1) * w] = p_ref[k, 0].astype(f32)
            b_ref[:, at * w : (at + 1) * w] = p_ref[k, 1].astype(f32)

    full = lambda d: pl.BlockSpec(d, lambda i: (0,) * len(d))
    return call(
        kernel, name, (parts,), in_specs=[full(parts.shape)], out_specs=[full((r, n * w))] * 2,
        out_shape=[shape((r, n * w), f32)] * 2,
    )


def shards(
    tokens,
    segments,
    norm1_gain,
    w_query,
    w_key,
    w_value,
    w_output,
    norm2_gain,
    w_gate,
    w_up,
    w_down,
    cotangent,
):
    mv = Moves()
    nz, z, ny, nb = mv.nz, mv.z, mv.ny, mv.nb
    n_dev = nz * nb
    groups, L, D = tokens.shape
    hd = w_key.shape[1]
    FF = w_gate.shape[1]
    T = groups * L
    hops = (WINDOW + L - 1) // L
    hop = hops * L
    fq = FF // GROUP
    core, xb = mv.bit(1), mv.bit(2)
    quarter = core * 2 + xb
    scalar = lambda v: v.astype(jnp.int32).reshape(1)
    qi, yi, xi = scalar(quarter), scalar(mv.y), scalar(xb)
    paired = ny == 2
    quarter_of = lambda b: b % 2 * 2 + b // 2 % 2

    rows = tokens.reshape(T, D)
    cot = cotangent.reshape(T, D)
    others = [mv.shift(segments + 1, "z", range(nz), distance) for distance in range(1, nz)]
    cot1 = mv.flip(cot, 1)
    cot2 = mv.flip(cot, 2)
    every = jnp.concatenate([jnp.where(o == 0, big, o) for o in others] + [segments + 1], axis=1)
    starts = jnp.sum((every[:, None, :] <= segments[:, :, None]).astype(jnp.int32), axis=2)
    index = z * L + jnp.arange(L, dtype=jnp.int32)
    positions = (index[None, :] - starts).astype(f32).reshape(T, 1)
    starts_rel = (starts - z * L + hop).reshape(T, 1)
    half = hd // 2
    freq = jnp.exp(-math.log(rope_base) * jnp.arange(half, dtype=f32) / half)
    angle = positions * freq
    cos_half, sin_half = jnp.cos(angle), jnp.sin(angle)
    cosine = jnp.concatenate([cos_half, cos_half], axis=1)
    sine = jnp.concatenate([-sin_half, sin_half], axis=1)

    normed, inv1, kv = norm_keys(rows, norm1_gain, w_key, w_value, cosine, sine)
    kv = kv.reshape(groups, L, 2 * hd)
    blocks = [kv]
    for _ in range(hops):
        blocks.insert(0, mv.shift(blocks[0], "z", range(nz), 1))
    kv_all = jnp.concatenate(blocks, axis=1)
    q_lin = project_query(normed, w_query, (kv,))
    attended, queries, lses = attention(q_lin, cosine, sine, starts_rel, kv_all, hop)
    mid, normed2, inv2 = project_out(attended, w_output, rows, norm2_gain, (cot1,))
    cot2 = hold(cot2, (normed2,))
    cot3 = mv.flip(cot2, 1)

    def of_group(v):
        far = mv.flip(v, GROUP)
        return v, mv.flip(v, 1), far, mv.flip(far, 1)

    normed_all, attended_all = (of_group(normed), of_group(attended)) if paired else ((), ())

    n1 = mv.flip(normed2, 1)
    n2 = mv.flip(normed2, 2)
    d_hidden = down_back(qi, (cot, cot1, cot2, cot3), w_down, (normed2,))
    h_a, dg_a, du_a = feed(qi, (normed2, n1), d_hidden, 0, w_gate, w_up, normed_all[1:])
    n2 = hold(n2, (du_a,))
    n3 = mv.flip(n2, 1)
    h_b, dg_b, du_b = feed(qi, (n2, n3), d_hidden, 2 * T, w_gate, w_up, (du_a,))
    n_all, c_all = (normed2, n1, n2, n3), (cot, cot1, cot2, cot3)
    same_quarter = [[k * GROUP + q for k in range(nz * ny)] for q in range(GROUP)]

    def sum_all(grad):
        return lax.psum_scatter(grad, AXES, scatter_dimension=0, tiled=True, axis_index_groups=same_quarter)

    def send_rows(name, d_a, d_b, deps):
        if not paired:
            return rows_product(name, n_all, d_a, d_b, 0 * yi, (D // 256, 1), None, deps), None
        part = rows_product(name, n_all, d_a, d_b, 1 - yi, (nz, 2), None, deps)
        return part, mv.flip(part, GROUP)

    def keep_rows(name, sent, d_a, d_b, deps):
        if not paired:
            return sent[0], sum_all(sent[0].reshape(D, fq))[None]
        part = rows_product(name, n_all, d_a, d_b, yi, (nz, 2), sent[1], deps)
        return part, lax.psum_scatter(part, "seq", scatter_dimension=0, tiled=True)

    dn_pairs = [[dg_a, dg_b], [du_a, du_b]]
    halves = 2 if paired else 1
    first_half = 1 - yi if paired else 0 * yi
    up_sent = send_rows("up_send", du_a, du_b, (du_b,) + attended_all[1:])
    g_gate = rows_product("gate", n_all, dg_a, dg_b, 0 * yi, (D // 256, 1), None, (up_sent[0],))
    dg_a = hold(dg_a, (g_gate,))
    dn_pairs = [[dg_a, dg_b], [du_a, du_b]]
    dn_away = partial_away("dn2_away", qi, dn_pairs, [w_gate, w_up], 1, ())
    dn_got = mv.flip(dn_away, 1)
    down_sent = columns_product("down_send", h_a, h_b, c_all, first_half, halves, None, (dn_away,))
    dn_far, dn_own = partial_near("dn2_near", qi, dn_pairs, [w_gate, w_up], 1, dn_got, (down_sent,))
    dn_last = mv.flip(dn_far, 2)
    out_away = partial_away("out_away", qi, [[h_a, h_b]], [w_down], 0, (dn_far,))
    out_got = mv.flip(out_away, 1)
    g_gate = g_gate.reshape(D, fq)
    if paired:
        down_got = mv.flip(down_sent, GROUP)
        z_gate = lax.psum_scatter(g_gate, "seq", scatter_dimension=0, tiled=True)
    else:
        z_gate = sum_all(g_gate)
    up_kept, r_up = keep_rows("up_keep", up_sent, du_a, du_b, (out_away,))
    out_far, out_own = partial_near("out_near", qi, [[h_a, h_b]], [w_down], 0, out_got, (up_kept,))
    out_last = mv.flip(out_far, 2)
    d_branch, norm2_term, d_attended = mid_back(
        dn_own, dn_last, mid, inv2, cot, norm2_gain, w_output, (out_far,)
    )

    def quarters(d):
        w = D // GROUP
        at = core * 2 + mv.y
        return [lax.dynamic_slice_in_dim(d, (at ^ k) * w, w, 1) for k in (0, 2, 1, 3)]

    def exchange(cuts):
        return cuts[0], mv.flip(cuts[1], 1), mv.flip(cuts[2], GROUP), mv.flip(cuts[3], GROUP + 1)

    db_cuts = quarters(d_branch) if paired else ()
    db_all = exchange(db_cuts) if paired else ()
    d_query, dkv_all = attention_back(
        queries, attended, d_attended, lses, cosine, sine, starts_rel, kv_all, hop, db_cuts
    )
    parts = [dkv_all[:, k * L : (k + 1) * L].astype(bf16) for k in range(hops)]
    back = mv.shift(parts[0], "z", range(nz), -1)
    if paired:
        dq_all = exchange(quarters(d_query))
        down_kept = columns_product(
            "down_keep", h_a, h_b, c_all, yi, 2, down_got, (d_query, z_gate) + tuple(db_all[1:2])
        )
        r_down = lax.psum_scatter(down_kept, "seq", scatter_dimension=0, tiled=True)
        last = down_kept
    else:
        r_gate, last = z_gate[None], d_query
    output = final_output(mid, out_own, out_last, (last,))
    last = output
    if paired:
        z_gate = hold(z_gate, (output,)).reshape(2, D // (2 * nz), fq)
        gate_away = mv.flip(lax.dynamic_index_in_dim(z_gate, 1 - mv.y, 0, keepdims=False), GROUP)
    back = hold(back, (last,))
    for part in parts[1:]:
        back = mv.shift((back.astype(f32) + part.astype(f32)).astype(bf16), "z", range(nz), -1)
    if paired:
        out_sent = token_products("w_out_send", attended_all, db_all, 1 - xi, None, (last, r_up) + dq_all[1:])
        out_recv = mv.flip(out_sent, 2)
        query_sent = token_products("w_query_send", normed_all, dq_all, 1 - xi, None, (out_sent,))
        query_recv = mv.flip(query_sent, 2)
        back = hold(back, (query_sent,))
        last = query_sent
    own = dkv_all[:, hop:] + back.astype(f32)
    own = own.reshape(T, 2 * hd)
    swapped = jnp.concatenate([own[:, half:hd], own[:, :half]], axis=1)
    d_key = (own[:, :hd] * cosine - swapped * sine).astype(bf16)
    d_kv = jnp.concatenate([d_key, own[:, hd:].astype(bf16)], axis=1)
    grad_tokens, norm1_term = tokens_back(
        d_query, d_kv, w_query, w_key, w_value, d_branch, rows, inv1, norm1_gain, (last,)
    )
    g_kv = dot(normed, d_kv, 0, 0, bf16)
    if paired:
        terms = jnp.concatenate([norm1_term, norm2_term, jnp.zeros((126, D), f32)], axis=0).T
        size = D // n_dev
        g_kv = jnp.concatenate([g_kv, terms.astype(bf16)], axis=1)
        g_kv = g_kv.reshape(nz, nb, size, 2 * hd + 128).transpose(1, 0, 2, 3)
        g_kv = lax.all_to_all(g_kv, "batch", 0, 0, tiled=True)
        g_out = token_products("w_out_keep", attended_all, db_all, xi, out_recv, (grad_tokens, r_down))
        r_out = lax.psum_scatter(g_out, "seq", scatter_dimension=0, tiled=True)
        g_query = token_products("w_query_keep", normed_all, dq_all, xi, query_recv, (g_out,))
        g_kv = hold(g_kv, (g_query,)) if HOLD_KV else g_kv
        g_kv = jnp.sum(g_kv.astype(f32), axis=0).astype(bf16)
        gate_away = hold(gate_away, (g_out,))
        gate_kept = lax.dynamic_index_in_dim(z_gate, mv.y, 0, keepdims=False)
        r_gate = (gate_kept.astype(f32) + gate_away.astype(f32)).astype(bf16)[None]
        joined = [
            g_query.reshape(nz, D // nz, D // nb),
            g_kv[:, :, : 2 * hd],
            jnp.pad(g_kv[:, :, 2 * hd :], ((0, 0), (0, 0), (0, D // nb - 128))),
        ]
        r_query = lax.psum_scatter(jnp.concatenate(joined, axis=1), "seq", scatter_dimension=0, tiled=True)[0]
        r_kv = r_query[D // nz : D // nz + size].astype(f32)
        norms = r_query[D // nz + size :, :2].astype(f32).T
        r_query = r_query[: D // nz]

        def finish(name, r):
            r = lax.all_to_all(r.reshape(nb, D // n_dev, D // nb), "batch", 0, 0, tiled=True)
            order = [y_ * GROUP + x_ * 2 + c_ for c_ in range(2) for y_ in range(2) for x_ in range(2)]
            return join_columns(name, r, order)

        grad_output, grad_query = finish("join_out", r_out), finish("join_query", r_query)
        r_down = r_down.reshape(2, fq // (2 * nz), D // 2)
        parts = []
        for k in range(2):
            pairs = [
                (z_ * nb + b_, quarter_of(b_) * ny * nz + (z_ * ny + b_ // GROUP) ^ k)
                for z_ in range(nz)
                for b_ in range(nb)
            ]
            piece = lax.dynamic_index_in_dim(r_down, mv.y ^ k, 0, keepdims=False)
            parts.append(lax.ppermute(piece, AXES, pairs))
        first = jnp.where(core == 0, parts[0], parts[1])
        second = jnp.where(core == 0, parts[1], parts[0])
        grad_down = jnp.concatenate([first, second], axis=1).astype(f32)
    else:
        r_kv = lax.psum_scatter(g_kv, AXES, scatter_dimension=0, tiled=True).astype(f32)
        norms = jnp.concatenate([norm1_term, norm2_term], axis=0)
        norms = norms.reshape(2, n_dev, D // n_dev).transpose(1, 0, 2)
        norms = jnp.sum(lax.all_to_all(norms, AXES, 0, 0, tiled=True), axis=0)
        r_down = sum_all(down_sent)
        pairs = [
            (z_ * nb + b_, quarter_of(b_) * ny * nz + z_ * ny + b_ // GROUP)
            for z_ in range(nz)
            for b_ in range(nb)
        ]
        grad_down = lax.ppermute(r_down, AXES, pairs).astype(f32)
        every_device = lambda g: lax.psum_scatter(g, AXES, scatter_dimension=0, tiled=True).astype(f32)
        grad_output = every_device(dot(attended, d_branch, 0, 0, bf16))
        grad_query = every_device(dot(normed, d_query, 0, 0, bf16))

    fours = [[k * GROUP + q for q in range(GROUP)] for k in range(ny)]

    def finish_quarter(r):
        k, height, width = r.shape
        r = r.reshape(k, GROUP, height // GROUP, width).transpose(1, 0, 2, 3)
        return lax.all_to_all(r, "batch", 0, 0, tiled=True, axis_index_groups=fours)

    gu = finish_quarter(jnp.concatenate([r_gate, r_up], axis=0))
    if paired:
        grad_gate, grad_up = join_two("join", gu, [quarter_of(i) for i in range(GROUP)])
    else:
        gu = jnp.stack([gu[quarter_of(i)] for i in range(GROUP)]).transpose(1, 2, 0, 3).reshape(2, D // n_dev, FF).astype(f32)
        grad_gate, grad_up = gu[0], gu[1]
    return (
        output.reshape(groups, L, D),
        grad_tokens.reshape(groups, L, D),
        norms[0],
        grad_query,
        r_kv[:, :hd],
        r_kv[:, hd:],
        grad_output,
        norms[1],
        grad_gate,
        grad_up,
        grad_down,
    )


def solution(mesh):
    data, vector, rows = P("batch", "seq", None), P(AXES), P(AXES, None)
    return jax.shard_map(
        shards,
        mesh=mesh,
        in_specs=(data, P("batch", "seq")) + (P(),) * 9 + (data,),
        out_specs=(data, data, vector, rows, rows, rows, rows, vector, rows, rows, rows),
        check_vma=False,
    )
```

```python
import functools
import math

import jax
import jax.numpy as jnp
from jax import lax
from jax.experimental import pallas as pl
from jax.experimental.pallas import tpu as pltpu
from jax.sharding import PartitionSpec as P

WINDOW = 512
eps = 1e-05
rope_base = 10000.0
masked = -1e30
big = 1 << 30
AXES = ("seq", "batch")
GROUP = 4
f32 = jnp.float32
bf16 = jnp.bfloat16


MIB = 2**20
ONCE = pl.Buffered(1)
ANY = pl.BlockSpec(memory_space=pl.ANY)
SCALE = 20.0
HOLD_KV = True
COST = dict(
    norm_keys=5, query=9, attend=14, project_out=11, down_back=20, feed=21, gate=19, gate_send=11, up_send=11, down_send=11,
    gate_keep=12, up_keep=12, down_keep=12, dn2_away=20, dn2_near=22, out_away=11, out_near=13, mid_back=14,
    attend_back=23, w_out_send=7, w_out_keep=7, w_query_send=7, w_query_keep=7, tokens_back=14, output=5, hold=1, join=1,
)


def call(kernel, name, args, deps=(), scalars=(), grid=(1,), in_specs=(), out_specs=None, out_shape=None, scratch=(), vmem=56, passes=()):
    n_s, n_a, n_d, n_p = len(scalars), len(args), len(deps), len(passes)
    several = isinstance(out_shape, (list, tuple))
    shapes, specs = (list(out_shape), list(out_specs)) if several else ([out_shape], [out_specs])
    n_o = len(shapes)

    def body(*refs):
        at = n_s + n_a + n_d + n_p
        kernel(*refs[: n_s + n_a], *refs[at : at + n_o], *refs[at + n_o + n_p :])

    out = pl.pallas_call(
        body,
        grid_spec=pltpu.PrefetchScalarGridSpec(
            num_scalar_prefetch=n_s,
            grid=grid,
            in_specs=list(in_specs) + [ANY] * (n_d + n_p),
            out_specs=specs + [ANY] * n_p,
            scratch_shapes=list(scratch),
        ),
        out_shape=shapes + [jax.ShapeDtypeStruct(p.shape, p.dtype) for p in passes],
        input_output_aliases={n_s + n_a + n_d + i: n_o + i for i in range(n_p)},
        compiler_params=pltpu.CompilerParams(vmem_limit_bytes=vmem * MIB),
        cost_estimate=pl.CostEstimate(flops=int(SCALE * COST.get(name, 1) * 10**9), bytes_accessed=1, transcendentals=0),
        name=name,
    )(*scalars, *args, *deps, *passes)
    return out if several or passes else out[0]


def dot(a, b, ca, cb, out=f32):
    return lax.dot_general(a, b, (((ca,), (cb,)), ((), ())), preferred_element_type=f32).astype(out)


class Moves:
    def __init__(self):
        self.nz, self.nb = lax.axis_size("seq"), lax.axis_size("batch")
        self.z, self.b = lax.axis_index("seq"), lax.axis_index("batch")
        self.ny = self.nb // GROUP
        self.y = self.b // GROUP

    def flip(self, value, mask):
        nz, nb = self.nz, self.nb
        pairs = [(z * nb + b, z * nb + (b ^ mask)) for z in range(nz) for b in range(nb)]
        return lax.ppermute(value, AXES, pairs)

    def shift(self, value, axis, sources, step):
        nz, ny, nb = self.nz, self.ny, self.nb
        pairs = []
        for z in range(nz):
            for b in range(nb):
                y, q = b // GROUP, b % GROUP
                at, size = (z, nz) if axis == "z" else (y, ny)
                if at in sources and 0 <= at + step < size:
                    to = (z + step, y) if axis == "z" else (z, y + step)
                    pairs.append((z * nb + b, to[0] * nb + to[1] * GROUP + q))
        return lax.ppermute(value, AXES, pairs)

    def bit(self, mask):
        return (self.b // mask) % 2


def turn(u, cosine, sine):
    return u * cosine + pltpu.roll(u, 64, 1) * sine


def mask_bias(starts, rows, first_row, keys, first_key, hop):
    qi = lax.broadcasted_iota(jnp.int32, (rows, keys), 0) + (first_row + hop)
    kj = lax.broadcasted_iota(jnp.int32, (rows, keys), 1) + first_key
    allow = (kj <= qi) & (qi - kj < WINDOW) & (kj >= starts)
    return jnp.where(allow, 0.0, masked)


def row_blocks(rows, block, hop):
    for r in range(0, rows, block):
        first = max(0, r + hop - WINDOW)
        first -= first % 128
        yield pl.ds(r, block), r, first, r + block + hop - first


def masked_scores(q, k, bias):
    rows, keys = bias.shape
    s = dot(q, k, 1, 1)
    return (s.reshape(s.shape[0] // rows, rows, keys) + bias[None]).reshape(s.shape)


def fwd_kernel(q_ref, cos_ref, sin_ref, start_ref, k_ref, v_ref, o_ref, qr_ref, lse_ref, *, hop):
    scale = math.log2(math.e) / math.sqrt(128)
    for sl, r, first, count in row_blocks(q_ref.shape[0], ROWS, hop):
        bias = mask_bias(start_ref[sl, :], ROWS, r, count, first, hop)
        cosine, sine = cos_ref[sl, :] * scale, sin_ref[sl, :] * scale
        kk, vv = k_ref[0, pl.ds(first, count), :], v_ref[0, pl.ds(first, count), :]
        for g in range(0, HEADS, TOGETHER):
            heads = range(g, g + TOGETHER)
            parts = []
            for h in heads:
                hs = pl.ds(h * 128, 128)
                part = turn(q_ref[sl, hs], cosine, sine).astype(bf16)
                qr_ref[sl, hs] = part
                parts.append(part)
            s = masked_scores(jnp.concatenate(parts, axis=0), kk, bias)
            top = jnp.max(s, axis=1, keepdims=True)
            e = jnp.exp2(s - top)
            total = jnp.sum(e, axis=1, keepdims=True)
            o = dot(e.astype(bf16), vv, 1, 0) * (1.0 / total)
            lse = top + jnp.log2(total)
            for i, h in enumerate(heads):
                at = slice(i * ROWS, (i + 1) * ROWS)
                o_ref[sl, pl.ds(h * 128, 128)] = o[at].astype(bf16)
                lse_ref[0, 0, sl, h : h + 1] = lse[at]


def bwd_kernel(q_ref, o_ref, do_ref, lse_ref, cos_ref, sin_ref, start_ref, k_ref, v_ref, dq_ref, dkv_ref, *, hop):
    scale = 1.0 / math.sqrt(128)

    @pl.when(pl.program_id(1) == 0)
    def _():
        dkv_ref[...] = jnp.zeros_like(dkv_ref)

    for sl, r, first, count in row_blocks(q_ref.shape[0], ROWS, hop):
        ks = pl.ds(first, count)
        bias = mask_bias(start_ref[sl, :], ROWS, r, count, first, hop)
        cosine, sine = cos_ref[sl, :] * scale, sin_ref[sl, :] * scale
        kk, vv = k_ref[0, ks, :], v_ref[0, ks, :]
        dk = dv = None
        for g in range(0, HEADS, TOGETHER):
            heads = range(g, g + TOGETHER)
            of = lambda ref: [ref[sl, pl.ds(h * 128, 128)] for h in heads]
            q, do = jnp.concatenate(of(q_ref), axis=0), jnp.concatenate(of(do_ref), axis=0)
            o = jnp.concatenate(of(o_ref), axis=0)
            lse = jnp.concatenate([lse_ref[0, 0, sl, h : h + 1] for h in heads], axis=0)
            inner = jnp.sum(do.astype(f32) * o.astype(f32), axis=1, keepdims=True)
            p = jnp.exp2(masked_scores(q, kk, bias) - lse)
            ds = (p * (dot(do, vv, 1, 1) - inner)).astype(bf16)
            dq = dot(ds, kk, 1, 0)
            for i, h in enumerate(heads):
                dq_ref[sl, pl.ds(h * 128, 128)] = turn(dq[i * ROWS : (i + 1) * ROWS], cosine, -sine).astype(bf16)
            dk_part, dv_part = dot(ds, q, 0, 0), dot(p.astype(bf16), do, 0, 0)
            dk = dk_part if dk is None else dk + dk_part
            dv = dv_part if dv is None else dv + dv_part
        dkv_ref[0, ks, :128] += dk * (1.0 / math.log2(math.e))
        dkv_ref[0, ks, 128:] += dv


HEADS = 8
TOGETHER = 4
ROWS = 128


def attention_specs(L, span):
    wide = pl.BlockSpec((L, HEADS * 128), lambda s, h: (s, h))
    table = pl.BlockSpec((L, 128), lambda s, h: (s, 0))
    starts = pl.BlockSpec((L, 1), lambda s, h: (s, 0))
    keys = pl.BlockSpec((1, span, 128), lambda s, h: (s, 0, 0)), pl.BlockSpec((1, span, 128), lambda s, h: (s, 0, 1))
    lse = pl.BlockSpec((1, 1, L, HEADS), lambda s, h: (s, h, 0, 0))
    return wide, table, starts, keys, lse


def attention(q_lin, cosine, sine, starts, kv, hop, deps=()):
    T, width = q_lin.shape
    groups, span, _ = kv.shape
    L = T // groups
    wide, table, start, key, lse = attention_specs(L, span)
    steps = width // (HEADS * 128)
    return call(
        functools.partial(fwd_kernel, hop=hop),
        "attend",
        (q_lin, cosine, sine, starts, kv, kv),
        deps,
        grid=(groups, steps),
        in_specs=[wide, table, table, start, *key],
        out_specs=[wide, wide, lse],
        out_shape=[
            jax.ShapeDtypeStruct((T, width), bf16),
            jax.ShapeDtypeStruct((T, width), bf16),
            jax.ShapeDtypeStruct((groups, steps, L, HEADS), f32),
        ],
    )


def attention_back(queries, attended, d_attended, lses, cosine, sine, starts, kv, hop, deps=()):
    T, width = queries.shape
    groups, span, _ = kv.shape
    L = T // groups
    wide, table, start, key, lse = attention_specs(L, span)
    steps = width // (HEADS * 128)
    return call(
        functools.partial(bwd_kernel, hop=hop),
        "attend_back",
        (queries, attended, d_attended, lses, cosine, sine, starts, kv, kv),
        deps,
        grid=(groups, steps),
        in_specs=[wide, wide, wide, lse, table, table, start, *key],
        out_specs=[wide, pl.BlockSpec((1, span, 256), lambda s, h: (s, 0, 0))],
        out_shape=[
            jax.ShapeDtypeStruct((T, width), bf16),
            jax.ShapeDtypeStruct((groups, span, 256), f32),
        ],
    )


def whole(a):
    return pl.BlockSpec(a.shape, lambda *i: (0,) * a.ndim, pipeline_mode=ONCE)


def shape(dims, dtype=bf16):
    return jax.ShapeDtypeStruct(dims, dtype)


def hold(value, deps):
    [out] = call(lambda: None, "hold", (), deps, out_shape=[], out_specs=[], passes=(value,))
    return out


def norm_keys(tokens, gain, w_key, w_value):
    T, D = tokens.shape
    block = 128
    hd = w_key.shape[1]

    def kernel(x_ref, g_ref, wk_ref, wv_ref, n_ref, inv_ref, kv_ref):
        x = x_ref[...].astype(f32)
        inv = lax.rsqrt(jnp.mean(x * x, axis=1, keepdims=True) + eps)
        normed = (x * inv * g_ref[...]).astype(bf16)
        n_ref[...] = normed
        inv_ref[...] = inv
        kv_ref[:, :hd] = dot(normed, wk_ref[...], 1, 0)
        kv_ref[:, hd:] = dot(normed, wv_ref[...], 1, 0)

    row = lambda w: pl.BlockSpec((block, w), lambda i: (i, 0))
    return call(
        kernel, "norm_keys", (tokens, gain.reshape(1, D), w_key, w_value), grid=(T // block,),
        in_specs=[row(D), pl.BlockSpec((1, D), lambda i: (0, 0)), whole(w_key), whole(w_value)],
        out_specs=[row(D), row(1), row(2 * hd)],
        out_shape=[shape((T, D)), shape((T, 1), f32), shape((T, 2 * hd), f32)],
        vmem=56,
    )


def project_query(normed, w_query, deps=()):
    T, D = normed.shape
    N = w_query.shape[1]
    block = 512

    def kernel(a_ref, b_ref, o_ref):
        o_ref[...] = dot(a_ref[...], b_ref[...], 1, 0)

    return call(
        kernel, "query", (normed, w_query), deps, grid=(N // block,),
        in_specs=[whole(normed), pl.BlockSpec((D, block), lambda i: (0, i))],
        out_specs=pl.BlockSpec((T, block), lambda i: (0, i)),
        out_shape=shape((T, N), f32),
        vmem=56,
    )


def project_out(attended, w_output, x_rows, gain, deps=(), passes=()):
    T, D = x_rows.shape
    block = 512
    steps = D // block

    def kernel(a_ref, w_ref, x_ref, g_ref, mid_ref, n_ref, inv_ref, sq_ref):
        i = pl.program_id(0)
        part = x_ref[...].astype(f32) + dot(a_ref[...], w_ref[...], 1, 0)
        mid_ref[:, pl.ds(i * block, block)] = part
        sq = jnp.sum(part * part, axis=1, keepdims=True)

        @pl.when(i == 0)
        def _():
            sq_ref[...] = sq

        @pl.when(i > 0)
        def _():
            sq_ref[...] += sq

        @pl.when(i == steps - 1)
        def _():
            inv = lax.rsqrt(sq_ref[...] * (1.0 / D) + eps)
            inv_ref[...] = inv
            n_ref[...] = (mid_ref[...] * inv * g_ref[...]).astype(bf16)

    full = lambda w: pl.BlockSpec((T, w), lambda i: (0, 0))
    return call(
        kernel, "project_out", (attended, w_output, x_rows, gain.reshape(1, D)), deps, grid=(steps,),
        in_specs=[whole(attended), pl.BlockSpec((D, block), lambda i: (0, i)), pl.BlockSpec((T, block), lambda i: (0, i)), pl.BlockSpec((1, D), lambda i: (0, 0))],
        out_specs=[full(D), full(D), full(1)],
        out_shape=[shape((T, D), f32), shape((T, D)), shape((T, 1), f32)],
        scratch=[pltpu.VMEM((T, 1), f32)],
        passes=passes,
    )


def of_pieces(pieces, block, order=None, rows=None):
    order = order or range(len(pieces))
    rows = rows or [(0, p.shape[0]) for p in pieces]
    specs = [None] * len(pieces)
    starts, at = [None] * len(pieces), 0
    for k in order:
        first, n = rows[k][0] // block, rows[k][1] // block
        specs[k] = pl.BlockSpec(
            (block, pieces[k].shape[1]),
            lambda i, *s, at=at, first=first, n=n: (first + jnp.clip(i - at, 0, n - 1), 0),
        )
        starts[k] = at
        at += n
    order = list(order)

    def read(refs):
        i = pl.program_id(0)
        value = refs[order[0]][...]
        for k in order[1:]:
            value = jnp.where(i >= starts[k], refs[k][...], value)
        return value

    return specs, read, at


def quarter_columns(w):
    return pl.BlockSpec((w.shape[0], w.shape[1] // GROUP), lambda i, q: (0, q[0]), pipeline_mode=ONCE)


def quarter_rows(w):
    return pl.BlockSpec((w.shape[0] // GROUP, w.shape[1]), lambda i, q: (q[0], 0), pipeline_mode=ONCE)


def down_back(quarter, pieces, w_down, deps=()):
    block = 256
    fq = w_down.shape[0] // GROUP
    n = len(pieces)
    specs, read, steps = of_pieces(pieces, block)

    def kernel(q_ref, *refs):
        refs[n + 1][...] = dot(read(refs[:n]), refs[n][...], 1, 1, bf16)

    return call(
        kernel, "down_back", (*pieces, w_down), deps, (quarter,), grid=(steps,),
        in_specs=specs + [quarter_rows(w_down)],
        out_specs=pl.BlockSpec((block, fq), lambda i, q: (i, 0)),
        out_shape=shape((steps * block, fq)),
        vmem=56,
    )


def feed(quarter, pieces, d_hidden, first, w_gate, w_up, deps=(), passes=()):
    block = 256
    fq = w_gate.shape[1] // GROUP
    n = len(pieces)
    specs, read, steps = of_pieces(pieces, block)
    first = first // block

    def kernel(q_ref, *refs):
        dh_ref, wg_ref, wu_ref, h_ref, dg_ref, du_ref = refs[n:]
        value = read(refs[:n])
        gate = dot(value, wg_ref[...], 1, 0)
        up = dot(value, wu_ref[...], 1, 0)
        dh = dh_ref[...].astype(f32)
        sig = jax.nn.sigmoid(gate)
        silu = gate * sig
        h_ref[...] = (silu * up).astype(bf16)
        dg_ref[...] = (dh * up * (sig + silu * (1.0 - sig))).astype(bf16)
        du_ref[...] = (dh * silu).astype(bf16)

    out = pl.BlockSpec((block, fq), lambda i, q: (i, 0))
    return call(
        kernel, "feed", (*pieces, d_hidden, w_gate, w_up), deps, (quarter,), grid=(steps,),
        in_specs=specs
        + [pl.BlockSpec((block, fq), lambda i, q: (i + first, 0)), quarter_columns(w_gate), quarter_columns(w_up)],
        out_specs=[out] * 3,
        out_shape=[shape((steps * block, fq))] * 3,
        passes=passes,
    )


def partial_away(name, quarter, pairs, weights, cb, deps=()):
    block = 256
    T = pairs[0][0].shape[0] // 2
    D = weights[0].shape[1 - cb]
    specs, reads = [], []
    for pair in pairs:
        s, read, steps = of_pieces(pair, block, rows=[(T, T)] * 2)
        specs += s
        reads.append(read)
    m = len(weights)

    def kernel(q_ref, *refs):
        total = None
        for j in range(m):
            part = dot(reads[j](refs[2 * j : 2 * j + 2]), refs[2 * m + j][...], 1, cb)
            total = part if total is None else total + part
        refs[-1][0] = total.astype(bf16)

    per = T // block
    return call(
        kernel, name, (*[p for g in pairs for p in g], *weights), deps, (quarter,), grid=(steps,),
        in_specs=specs + [quarter_columns(w) if cb else quarter_rows(w) for w in weights],
        out_specs=pl.BlockSpec((1, block, D), lambda i, q: (i // per, i % per, 0)),
        out_shape=shape((2, T, D)),
        vmem=56,
    )


def partial_near(name, quarter, pairs, weights, cb, got, deps=()):
    block = 256
    T = pairs[0][0].shape[0] // 2
    D = weights[0].shape[1 - cb]
    per = T // block
    specs, reads = [], []
    for pair in pairs:
        s, read, steps = of_pieces(pair, block, order=(1, 0), rows=[(0, T)] * 2)
        specs += s
        reads.append(read)
    m = len(weights)

    def kernel(q_ref, *refs):
        got_ref, far_ref, own_ref = refs[3 * m :]
        total = got_ref[0].astype(f32)
        for j in range(m):
            total = total + dot(reads[j](refs[2 * j : 2 * j + 2]), refs[2 * m + j][...], 1, cb)
        i = pl.program_id(0)

        @pl.when(i < per)
        def _():
            far_ref[...] = total.astype(bf16)

        @pl.when(i >= per)
        def _():
            own_ref[...] = total.astype(bf16)

    return call(
        kernel, name, (*[p for g in pairs for p in g], *weights, got), deps, (quarter,), grid=(steps,),
        in_specs=specs
        + [quarter_columns(w) if cb else quarter_rows(w) for w in weights]
        + [pl.BlockSpec((1, block, D), lambda i, q: (1 - i // per, i % per, 0))],
        out_specs=[
            pl.BlockSpec((block, D), lambda i, q: (jnp.minimum(i, per - 1), 0)),
            pl.BlockSpec((block, D), lambda i, q: (jnp.maximum(i - per, 0), 0)),
        ],
        out_shape=[shape((T, D))] * 2,
        vmem=56,
    )


def rows_product(name, n_all, d_a, d_b, half, parts, got=None, deps=()):
    D, fq = n_all[0].shape[1], d_a.shape[1]
    T = n_all[0].shape[0]
    blocks, halves = parts
    block = D // (blocks * halves)
    extra = () if got is None else (got,)

    def kernel(s_ref, n0, n1, n2, n3, a_ref, b_ref, *rest):
        total = dot(n0[...], a_ref[:T], 0, 0) + dot(n1[...], a_ref[T:], 0, 0)
        total = total + dot(n2[...], b_ref[:T], 0, 0) + dot(n3[...], b_ref[T:], 0, 0)
        if extra:
            total = total + rest[0][0].astype(f32)
        rest[-1][0] = total.astype(bf16)

    cut = pl.BlockSpec((T, block), lambda i, s: (0, i * halves + s[0]))
    out = pl.BlockSpec((1, block, fq), lambda i, s: (i, 0, 0))
    return call(
        kernel, name, (*n_all, d_a, d_b, *extra), deps, (half,), grid=(blocks,),
        in_specs=[cut] * 4 + [whole(d_a), whole(d_b)] + [out] * len(extra),
        out_specs=out,
        out_shape=shape((blocks, block, fq)),
        vmem=56,
    )


def columns_product(name, h_a, h_b, c_all, half, halves, got=None, deps=()):
    D, fq = c_all[0].shape[1], h_a.shape[1]
    T = c_all[0].shape[0]
    block = 256
    steps = D // halves // block
    extra = () if got is None else (got,)

    def kernel(s_ref, c0, c1, c2, c3, a_ref, b_ref, *rest):
        total = dot(a_ref[:T], c0[...], 0, 0) + dot(a_ref[T:], c1[...], 0, 0)
        total = total + dot(b_ref[:T], c2[...], 0, 0) + dot(b_ref[T:], c3[...], 0, 0)
        if extra:
            total = total + rest[0][...].astype(f32)
        rest[-1][...] = total.astype(bf16)

    cut = pl.BlockSpec((T, block), lambda i, s: (0, s[0] * steps + i))
    out = pl.BlockSpec((fq, block), lambda i, s: (0, i))
    return call(
        kernel, name, (*c_all, h_a, h_b, *extra), deps, (half,), grid=(steps,),
        in_specs=[cut] * 4 + [whole(h_a), whole(h_b)] + [out] * len(extra),
        out_specs=out,
        out_shape=shape((fq, D // halves)),
        vmem=56,
    )


def token_products(name, rows, d_all, half, got=None, deps=(), passes=()):
    T, M = rows[0].shape
    N = d_all[0].shape[1] // 2
    block = 512
    n = len(rows)
    extra = () if got is None else (got,)

    def kernel(s_ref, *refs):
        total = dot(refs[0][...], refs[n][...], 0, 0)
        for i in range(1, n):
            total = total + dot(refs[i][...], refs[n + i][...], 0, 0)
        if extra:
            total = total + refs[2 * n][...].astype(f32)
        refs[-1][...] = total.astype(bf16)

    cut = pl.BlockSpec((T, block), lambda i, s: (0, i))
    col = pl.BlockSpec((T, N), lambda i, s: (0, s[0]), pipeline_mode=ONCE)
    out = pl.BlockSpec((block, N), lambda i, s: (i, 0))
    return call(
        kernel, name, (*rows, *d_all, *extra), deps, (half,), grid=(M // block,),
        in_specs=[cut] * n + [col] * n + [out] * len(extra),
        out_specs=out,
        out_shape=shape((M, N)),
        passes=passes,
    )


def mid_back(own, got, mid, inverse, cot, gain, w_output, deps=()):
    T, D = mid.shape
    C = w_output.shape[0]
    block, rows = 512, 128

    def kernel(o_ref, g_ref, m_ref, i_ref, c_ref, gain_ref, w_ref, b_ref, n_ref, a_ref):
        @pl.when(pl.program_id(0) == 0)
        def _():
            for r in range(T // rows):
                sl = pl.ds(r * rows, rows)
                dn = o_ref[sl].astype(f32) + g_ref[sl].astype(f32)
                m, inv = m_ref[sl], i_ref[sl]
                mi = m * inv
                grad = jnp.sum(dn * mi, axis=0, keepdims=True)
                if r == 0:
                    n_ref[...] = grad
                else:
                    n_ref[...] += grad
                e = dn * gain_ref[...]
                mean = jnp.mean(e * mi, axis=1, keepdims=True)
                b_ref[sl] = (c_ref[sl].astype(f32) + inv * (e - mi * mean)).astype(bf16)

        a_ref[...] = dot(b_ref[...], w_ref[...], 1, 1, bf16)

    full = lambda w: pl.BlockSpec((T, w), lambda i: (0, 0))
    vec = pl.BlockSpec((1, D), lambda i: (0, 0))
    return call(
        kernel, "mid_back", (own, got, mid, inverse, cot, gain.reshape(1, D), w_output), deps, grid=(C // block,),
        in_specs=[whole(own), whole(got), whole(mid), full(1), whole(cot), vec, pl.BlockSpec((block, D), lambda i: (i, 0))],
        out_specs=[full(D), vec, pl.BlockSpec((T, block), lambda i: (0, i))],
        out_shape=[shape((T, D)), shape((1, D), f32), shape((T, C))],
        vmem=56,
    )


def tokens_back(d_query, d_kv, w_query, w_key, w_value, d_branch, tokens, inverse, gain, deps=()):
    T, D = tokens.shape
    block, rows = 512, 128
    hd = w_key.shape[1]
    steps = D // block

    def kernel(q_ref, kv_ref, wq_ref, wk_ref, wv_ref, b_ref, x_ref, i_ref, gain_ref, t_ref, n_ref, sum_ref):
        i = pl.program_id(0)
        at = pl.ds(i * block, block)
        inv = i_ref[...]
        dn = dot(q_ref[...], wq_ref[...], 1, 1)
        dn = dn + dot(kv_ref[:, :hd], wk_ref[...], 1, 1) + dot(kv_ref[:, hd:], wv_ref[...], 1, 1)
        xi = x_ref[...].astype(f32) * inv
        n_ref[...] = jnp.sum(dn * xi, axis=0, keepdims=True)
        e = dn * gain_ref[...]
        t_ref[:, at] = e
        part = jnp.sum(e * xi, axis=1, keepdims=True)

        @pl.when(i == 0)
        def _():
            sum_ref[...] = part

        @pl.when(i > 0)
        def _():
            sum_ref[...] += part

        @pl.when(i == steps - 1)
        def _():
            for r in range(T // rows):
                sl = pl.ds(r * rows, rows)
                iv = i_ref[sl]
                mean = sum_ref[sl] * (1.0 / D)
                t_ref[sl] = b_ref[sl].astype(f32) + iv * (t_ref[sl] - x_full[0][sl].astype(f32) * iv * mean)

    x_full = [None]

    def outer(q_ref, kv_ref, wq_ref, wk_ref, wv_ref, b_ref, x_ref, xf_ref, i_ref, gain_ref, t_ref, n_ref, sum_ref):
        x_full[0] = xf_ref
        kernel(q_ref, kv_ref, wq_ref, wk_ref, wv_ref, b_ref, x_ref, i_ref, gain_ref, t_ref, n_ref, sum_ref)

    full = lambda w: pl.BlockSpec((T, w), lambda i: (0, 0))
    vec = pl.BlockSpec((1, block), lambda i: (0, i))
    return call(
        outer, "tokens_back", (d_query, d_kv, w_query, w_key, w_value, d_branch, tokens, tokens, inverse, gain.reshape(1, D)), deps, grid=(steps,),
        in_specs=[
            whole(d_query), whole(d_kv), pl.BlockSpec((block, w_query.shape[1]), lambda i: (i, 0)),
            pl.BlockSpec((block, hd), lambda i: (i, 0)), pl.BlockSpec((block, hd), lambda i: (i, 0)), whole(d_branch),
            pl.BlockSpec((T, block), lambda i: (0, i)), whole(tokens), full(1), vec,
        ],
        out_specs=[full(D), vec],
        out_shape=[shape((T, D), f32), shape((1, D), f32)],
        scratch=[pltpu.VMEM((T, 1), f32)],
        vmem=56,
    )


def final_output(mid, own, got, deps=()):
    T, D = mid.shape
    block = 128

    def kernel(m_ref, a_ref, b_ref, o_ref):
        o_ref[...] = (m_ref[...] + a_ref[...].astype(f32) + b_ref[...].astype(f32)).astype(bf16)

    row = pl.BlockSpec((block, D), lambda i: (i, 0))
    return call(
        kernel, "output", (mid, own, got), deps, grid=(T // block,), in_specs=[row] * 3, out_specs=row,
        out_shape=shape((T, D)), vmem=56,
    )


def join_columns(name, parts, order):
    n, r, w = parts.shape

    def kernel(p_ref, o_ref):
        for k, b in enumerate(order):
            o_ref[:, k * w : (k + 1) * w] = p_ref[b].astype(f32)

    full = lambda d: pl.BlockSpec(d, lambda i: (0,) * len(d))
    return call(kernel, name, (parts,), in_specs=[full(parts.shape)], out_specs=full((r, n * w)), out_shape=shape((r, n * w), f32))


def join_two(name, parts, order):
    n, _, r, w = parts.shape

    def kernel(p_ref, a_ref, b_ref):
        for k, at in enumerate(order):
            a_ref[:, at * w : (at + 1) * w] = p_ref[k, 0].astype(f32)
            b_ref[:, at * w : (at + 1) * w] = p_ref[k, 1].astype(f32)

    full = lambda d: pl.BlockSpec(d, lambda i: (0,) * len(d))
    return call(
        kernel, name, (parts,), in_specs=[full(parts.shape)], out_specs=[full((r, n * w))] * 2,
        out_shape=[shape((r, n * w), f32)] * 2,
    )


def shards(
    tokens,
    segments,
    norm1_gain,
    w_query,
    w_key,
    w_value,
    w_output,
    norm2_gain,
    w_gate,
    w_up,
    w_down,
    cotangent,
):
    mv = Moves()
    nz, z, ny, nb = mv.nz, mv.z, mv.ny, mv.nb
    n_dev = nz * nb
    groups, L, D = tokens.shape
    hd = w_key.shape[1]
    FF = w_gate.shape[1]
    T = groups * L
    hops = (WINDOW + L - 1) // L
    hop = hops * L
    fq = FF // GROUP
    core, xb = mv.bit(1), mv.bit(2)
    quarter = core * 2 + xb
    scalar = lambda v: v.astype(jnp.int32).reshape(1)
    qi, yi, xi = scalar(quarter), scalar(mv.y), scalar(xb)
    paired = ny == 2
    quarter_of = lambda b: b % 2 * 2 + b // 2 % 2

    rows = tokens.reshape(T, D)
    cot = cotangent.reshape(T, D)
    others = [mv.shift(segments + 1, "z", range(nz), distance) for distance in range(1, nz)]
    cot1 = mv.flip(cot, 1)
    cot2 = mv.flip(cot, 2)
    every = jnp.concatenate([jnp.where(o == 0, big, o) for o in others] + [segments + 1], axis=1)
    starts = jnp.sum((every[:, None, :] <= segments[:, :, None]).astype(jnp.int32), axis=2)
    index = z * L + jnp.arange(L, dtype=jnp.int32)
    positions = (index[None, :] - starts).astype(f32).reshape(T, 1)
    starts_rel = (starts - z * L + hop).reshape(T, 1)
    half = hd // 2
    freq = jnp.exp(-math.log(rope_base) * jnp.arange(half, dtype=f32) / half)
    angle = positions * freq
    cos_half, sin_half = jnp.cos(angle), jnp.sin(angle)
    cosine = jnp.concatenate([cos_half, cos_half], axis=1)
    sine = jnp.concatenate([-sin_half, sin_half], axis=1)

    normed, inv1, kv = norm_keys(rows, norm1_gain, w_key, w_value)
    key_swapped = jnp.concatenate([kv[:, half:hd], kv[:, :half]], axis=1)
    kv = jnp.concatenate([kv[:, :hd] * cosine + key_swapped * sine, kv[:, hd:]], axis=1).astype(bf16)
    kv = kv.reshape(groups, L, 2 * hd)
    blocks = [kv]
    for _ in range(hops):
        blocks.insert(0, mv.shift(blocks[0], "z", range(nz), 1))
    kv_all = jnp.concatenate(blocks, axis=1)
    q_lin = project_query(normed, w_query, (kv,))
    attended, queries, lses = attention(q_lin, cosine, sine, starts_rel, kv_all, hop)
    mid, normed2, inv2 = project_out(attended, w_output, rows, norm2_gain, (cot1,))
    cot2 = hold(cot2, (normed2,))
    cot3 = mv.flip(cot2, 1)

    def of_group(v):
        far = mv.flip(v, GROUP)
        return v, mv.flip(v, 1), far, mv.flip(far, 1)

    normed_all, attended_all = (of_group(normed), of_group(attended)) if paired else ((), ())

    n1 = mv.flip(normed2, 1)
    n2 = mv.flip(normed2, 2)
    d_hidden = down_back(qi, (cot, cot1, cot2, cot3), w_down, (normed2,))
    h_a, dg_a, du_a = feed(qi, (normed2, n1), d_hidden, 0, w_gate, w_up, normed_all[1:])
    n2 = hold(n2, (du_a,))
    n3 = mv.flip(n2, 1)
    h_b, dg_b, du_b = feed(qi, (n2, n3), d_hidden, 2 * T, w_gate, w_up, (du_a,))
    n_all, c_all = (normed2, n1, n2, n3), (cot, cot1, cot2, cot3)
    same_quarter = [[k * GROUP + q for k in range(nz * ny)] for q in range(GROUP)]

    def sum_all(grad):
        return lax.psum_scatter(grad, AXES, scatter_dimension=0, tiled=True, axis_index_groups=same_quarter)

    def send_rows(name, d_a, d_b, deps):
        if not paired:
            return rows_product(name, n_all, d_a, d_b, 0 * yi, (D // 256, 1), None, deps), None
        part = rows_product(name, n_all, d_a, d_b, 1 - yi, (nz, 2), None, deps)
        return part, mv.flip(part, GROUP)

    def keep_rows(name, sent, d_a, d_b, deps):
        if not paired:
            return sent[0], sum_all(sent[0].reshape(D, fq))[None]
        part = rows_product(name, n_all, d_a, d_b, yi, (nz, 2), sent[1], deps)
        return part, lax.psum_scatter(part, "seq", scatter_dimension=0, tiled=True)

    dn_pairs = [[dg_a, dg_b], [du_a, du_b]]
    halves = 2 if paired else 1
    first_half = 1 - yi if paired else 0 * yi
    up_sent = send_rows("up_send", du_a, du_b, (du_b,) + attended_all[1:])
    g_gate = rows_product("gate", n_all, dg_a, dg_b, 0 * yi, (D // 256, 1), None, (up_sent[0],))
    dg_a = hold(dg_a, (g_gate,))
    dn_pairs = [[dg_a, dg_b], [du_a, du_b]]
    dn_away = partial_away("dn2_away", qi, dn_pairs, [w_gate, w_up], 1, ())
    dn_got = mv.flip(dn_away, 1)
    down_sent = columns_product("down_send", h_a, h_b, c_all, first_half, halves, None, (dn_away,))
    dn_far, dn_own = partial_near("dn2_near", qi, dn_pairs, [w_gate, w_up], 1, dn_got, (down_sent,))
    dn_last = mv.flip(dn_far, 2)
    out_away = partial_away("out_away", qi, [[h_a, h_b]], [w_down], 0, (dn_far,))
    out_got = mv.flip(out_away, 1)
    g_gate = g_gate.reshape(D, fq)
    if paired:
        down_got = mv.flip(down_sent, GROUP)
        z_gate = lax.psum_scatter(g_gate, "seq", scatter_dimension=0, tiled=True)
    else:
        z_gate = sum_all(g_gate)
    up_kept, r_up = keep_rows("up_keep", up_sent, du_a, du_b, (out_away,))
    out_far, out_own = partial_near("out_near", qi, [[h_a, h_b]], [w_down], 0, out_got, (up_kept,))
    out_last = mv.flip(out_far, 2)
    d_branch, norm2_term, d_attended = mid_back(
        dn_own, dn_last, mid, inv2, cot, norm2_gain, w_output, (out_far,)
    )

    def quarters(d):
        w = D // GROUP
        at = core * 2 + mv.y
        return [lax.dynamic_slice_in_dim(d, (at ^ k) * w, w, 1) for k in (0, 2, 1, 3)]

    def exchange(cuts):
        return cuts[0], mv.flip(cuts[1], 1), mv.flip(cuts[2], GROUP), mv.flip(cuts[3], GROUP + 1)

    db_cuts = quarters(d_branch) if paired else ()
    db_all = exchange(db_cuts) if paired else ()
    d_query, dkv_all = attention_back(
        queries, attended, d_attended, lses, cosine, sine, starts_rel, kv_all, hop, db_cuts
    )
    parts = [dkv_all[:, k * L : (k + 1) * L].astype(bf16) for k in range(hops)]
    back = mv.shift(parts[0], "z", range(nz), -1)
    if paired:
        dq_all = exchange(quarters(d_query))
        down_kept = columns_product(
            "down_keep", h_a, h_b, c_all, yi, 2, down_got, (d_query, z_gate) + tuple(db_all[1:2])
        )
        r_down = lax.psum_scatter(down_kept, "seq", scatter_dimension=0, tiled=True)
        last = down_kept
    else:
        r_gate, last = z_gate[None], d_query
    output = final_output(mid, out_own, out_last, (last,))
    last = output
    if paired:
        z_gate = hold(z_gate, (output,)).reshape(2, D // (2 * nz), fq)
        gate_away = mv.flip(lax.dynamic_index_in_dim(z_gate, 1 - mv.y, 0, keepdims=False), GROUP)
    back = hold(back, (last,))
    for part in parts[1:]:
        back = mv.shift((back.astype(f32) + part.astype(f32)).astype(bf16), "z", range(nz), -1)
    if paired:
        out_sent = token_products("w_out_send", attended_all, db_all, 1 - xi, None, (last, r_up) + dq_all[1:])
        out_recv = mv.flip(out_sent, 2)
        query_sent = token_products("w_query_send", normed_all, dq_all, 1 - xi, None, (out_sent,))
        query_recv = mv.flip(query_sent, 2)
        back = hold(back, (query_sent,))
        last = query_sent
    own = dkv_all[:, hop:] + back.astype(f32)
    own = own.reshape(T, 2 * hd)
    swapped = jnp.concatenate([own[:, half:hd], own[:, :half]], axis=1)
    d_key = (own[:, :hd] * cosine - swapped * sine).astype(bf16)
    d_kv = jnp.concatenate([d_key, own[:, hd:].astype(bf16)], axis=1)
    grad_tokens, norm1_term = tokens_back(
        d_query, d_kv, w_query, w_key, w_value, d_branch, rows, inv1, norm1_gain, (last,)
    )
    g_kv = dot(normed, d_kv, 0, 0, bf16)
    if paired:
        terms = jnp.concatenate([norm1_term, norm2_term, jnp.zeros((126, D), f32)], axis=0).T
        size = D // n_dev
        g_kv = jnp.concatenate([g_kv, terms.astype(bf16)], axis=1)
        g_kv = g_kv.reshape(nz, nb, size, 2 * hd + 128).transpose(1, 0, 2, 3)
        g_kv = lax.all_to_all(g_kv, "batch", 0, 0, tiled=True)
        g_out = token_products("w_out_keep", attended_all, db_all, xi, out_recv, (grad_tokens, r_down))
        r_out = lax.psum_scatter(g_out, "seq", scatter_dimension=0, tiled=True)
        g_query = token_products("w_query_keep", normed_all, dq_all, xi, query_recv, (g_out,))
        g_kv = hold(g_kv, (g_query,)) if HOLD_KV else g_kv
        g_kv = jnp.sum(g_kv.astype(f32), axis=0).astype(bf16)
        gate_away = hold(gate_away, (g_out,))
        gate_kept = lax.dynamic_index_in_dim(z_gate, mv.y, 0, keepdims=False)
        r_gate = (gate_kept.astype(f32) + gate_away.astype(f32)).astype(bf16)[None]
        joined = [
            g_query.reshape(nz, D // nz, D // nb),
            g_kv[:, :, : 2 * hd],
            jnp.pad(g_kv[:, :, 2 * hd :], ((0, 0), (0, 0), (0, D // nb - 128))),
        ]
        r_query = lax.psum_scatter(jnp.concatenate(joined, axis=1), "seq", scatter_dimension=0, tiled=True)[0]
        r_kv = r_query[D // nz : D // nz + size].astype(f32)
        norms = r_query[D // nz + size :, :2].astype(f32).T
        r_query = r_query[: D // nz]

        def finish(name, r):
            r = lax.all_to_all(r.reshape(nb, D // n_dev, D // nb), "batch", 0, 0, tiled=True)
            order = [y_ * GROUP + x_ * 2 + c_ for c_ in range(2) for y_ in range(2) for x_ in range(2)]
            return join_columns(name, r, order)

        grad_output, grad_query = finish("join_out", r_out), finish("join_query", r_query)
        r_down = r_down.reshape(2, fq // (2 * nz), D // 2)
        parts = []
        for k in range(2):
            pairs = [
                (z_ * nb + b_, quarter_of(b_) * ny * nz + (z_ * ny + b_ // GROUP) ^ k)
                for z_ in range(nz)
                for b_ in range(nb)
            ]
            piece = lax.dynamic_index_in_dim(r_down, mv.y ^ k, 0, keepdims=False)
            parts.append(lax.ppermute(piece, AXES, pairs))
        first = jnp.where(core == 0, parts[0], parts[1])
        second = jnp.where(core == 0, parts[1], parts[0])
        grad_down = jnp.concatenate([first, second], axis=1).astype(f32)
    else:
        r_kv = lax.psum_scatter(g_kv, AXES, scatter_dimension=0, tiled=True).astype(f32)
        norms = jnp.concatenate([norm1_term, norm2_term], axis=0)
        norms = norms.reshape(2, n_dev, D // n_dev).transpose(1, 0, 2)
        norms = jnp.sum(lax.all_to_all(norms, AXES, 0, 0, tiled=True), axis=0)
        r_down = sum_all(down_sent)
        pairs = [
            (z_ * nb + b_, quarter_of(b_) * ny * nz + z_ * ny + b_ // GROUP)
            for z_ in range(nz)
            for b_ in range(nb)
        ]
        grad_down = lax.ppermute(r_down, AXES, pairs).astype(f32)
        every_device = lambda g: lax.psum_scatter(g, AXES, scatter_dimension=0, tiled=True).astype(f32)
        grad_output = every_device(dot(attended, d_branch, 0, 0, bf16))
        grad_query = every_device(dot(normed, d_query, 0, 0, bf16))

    fours = [[k * GROUP + q for q in range(GROUP)] for k in range(ny)]

    def finish_quarter(r):
        k, height, width = r.shape
        r = r.reshape(k, GROUP, height // GROUP, width).transpose(1, 0, 2, 3)
        return lax.all_to_all(r, "batch", 0, 0, tiled=True, axis_index_groups=fours)

    gu = finish_quarter(jnp.concatenate([r_gate, r_up], axis=0))
    if paired:
        grad_gate, grad_up = join_two("join", gu, [quarter_of(i) for i in range(GROUP)])
    else:
        gu = jnp.stack([gu[quarter_of(i)] for i in range(GROUP)]).transpose(1, 2, 0, 3).reshape(2, D // n_dev, FF).astype(f32)
        grad_gate, grad_up = gu[0], gu[1]
    return (
        output.reshape(groups, L, D),
        grad_tokens.reshape(groups, L, D),
        norms[0],
        grad_query,
        r_kv[:, :hd],
        r_kv[:, hd:],
        grad_output,
        norms[1],
        grad_gate,
        grad_up,
        grad_down,
    )


def solution(mesh):
    data, vector, rows = P("batch", "seq", None), P(AXES), P(AXES, None)
    return jax.shard_map(
        shards,
        mesh=mesh,
        in_specs=(data, P("batch", "seq")) + (P(),) * 9 + (data,),
        out_specs=(data, data, vector, rows, rows, rows, rows, vector, rows, rows, rows),
        check_vma=False,
    )
```
